512 devices in a mesh: orient: 32 (over y_lo, z), brow: 2 (over core), bcol: 8 (over x, y_hi).
Axes of the slice: x: 4, y: 4 (y_hi: 2, y_lo: 2; y = y_hi * 2 + y_lo), z: 16, core: 2. Of those that a mesh axis runs over, the one named last changes fastest.
Arguments:
- volume: float32 [32, 64, 832], P('orient', 'brow', 'bcol'), may hold values from -700 to 700
- template: float32 [24, 24, 24], replicated, may hold values from 0 to 1
- voxel_maps: int32 [32, 13824], P('orient'), may hold values from 0 to 13823, as said below
Outputs:
- best: float32 [32, 64, 832], P('orient', 'brow', 'bcol')
The draws below stay inside these ranges and needn't reach their ends.
Inputs may be any that keep to these rules, and one draw needn't show every extreme that they name: `voxel_maps`: each row holds every number of 0 to 13823 exactly once.
All inputs are finite; a program needn't handle non-finite values.
Results may differ from the reference program's by a relative error of at most 0.00013.
Values sent between devices are 32-bit elements; how exact they have to be, the bound alone decides.
No kernel may reach another device: no remote copies, remote signals or barrier semaphores. Data moves between devices by JAX's collectives and lax.ppermute only.
A program may use at most 64 MiB of HBM per device.

```python
import math
import jax
import jax.numpy as jnp
from jax import lax

TS = 24
HALF = 12
VOX = 13824
NZ = 32
NX = 64
NY = 832
ROT = 32


def draw_volume(key, part):
    subkeys = jax.random.split(jax.random.fold_in(key, 17), 3)
    row_scale = jnp.exp(jax.random.uniform(subkeys[1], (NZ, NX, 1), minval=0.0, maxval=math.log(10.0)))
    col_scale = jnp.exp(jax.random.uniform(subkeys[2], (1, 1, NY), minval=0.0, maxval=math.log(10.0)))
    noise_part = jnp.clip(jax.random.normal(subkeys[0], (NZ, NX, NY)), -6.0, 6.0)
    samples = noise_part * row_scale * col_scale
    return samples.astype(jnp.float32)


def cycled_row(row_key):
    identity = jnp.arange(VOX, dtype=jnp.int32)
    order = jax.random.permutation(row_key, identity)
    moved_count = max(VOX // 16, 2)
    moved = order[:moved_count]
    targets = jnp.roll(moved, 1)
    return identity.at[moved].set(targets)


def draw_voxel_maps(key, part):
    row_keys = jax.random.split(jax.random.fold_in(key, 29), ROT)
    return jax.vmap(cycled_row)(row_keys).astype(jnp.int32)


def setup_inputs(seed: int = 0) -> dict:
    streams_of = jax.random.split(jax.random.key(seed), 4)
    volume = draw_volume(jax.random.fold_in(streams_of[3], 71), 0)
    template = jnp.clip(jax.random.uniform(streams_of[1], (TS, TS, TS), jnp.float32, 0.0, 1.0), 0.0, 1.0)
    voxel_maps = draw_voxel_maps(jax.random.fold_in(streams_of[3], 71), 0)
    return dict(volume=volume, template=template, voxel_maps=voxel_maps)


epsilon = 1e-06
floor_share = 0.1

def whiten_window(volume):
    spectrum = jnp.fft.fft(volume, axis=-1)
    power_spec = spectrum.real * spectrum.real + spectrum.imag * spectrum.imag
    smoothed = (jnp.roll(power_spec, 1, axis=-1) + power_spec + jnp.roll(power_spec, -1, axis=-1)) / 3.0
    smoothed = smoothed + floor_share * lax.optimization_barrier(jnp.mean(power_spec, axis=-1, keepdims=True)) + epsilon
    weights = lax.rsqrt(smoothed)
    return jnp.fft.ifft(spectrum * weights, axis=-1).real * math.sqrt(NY)

def reference(volume, template, voxel_maps):
    whitened = whiten_window(volume)
    padded = jnp.pad(whitened, HALF)
    flattened = template.reshape(-1)
    centred = flattened - jnp.mean(flattened)
    normed = centred / jnp.sqrt(jnp.sum(centred * centred) + epsilon)
    full_shape = padded.shape
    volume_spec = jnp.fft.fftn(padded)
    energy = lax.reduce_window(padded * padded, jnp.zeros((), padded.dtype), lax.add, (TS, TS, TS), (1, 1, 1), 'VALID')[:NZ, :NX, :NY]
    scaling = lax.rsqrt(energy / VOX + epsilon)

    def one_rotation(maximum, index_map):
        rotated = normed[index_map].reshape(TS, TS, TS)
        tpl_spec = jnp.fft.fftn(rotated, s=full_shape)
        correlation = jnp.fft.ifftn(volume_spec * jnp.conj(tpl_spec)).real[:NZ, :NX, :NY]
        return (jnp.maximum(maximum, correlation * scaling), None)
    initial = jnp.full((NZ, NX, NY), -jnp.inf, dtype=whitened.dtype)
    maximum, unused = lax.scan(one_rotation, initial, voxel_maps)
    return maximum
```

```python
import functools
import math

import jax
import jax.numpy as jnp
import ml_dtypes
import numpy as np
from jax import lax
from jax.experimental import pallas as pl
from jax.experimental.pallas import tpu as pltpu
from jax.sharding import Mesh
from jax.sharding import PartitionSpec as P

epsilon = 1e-06
floor_share = 0.1
edge = 24
half = 12
voxels = edge**3
length = 832
cols = 104
window = 128
rows = 32
planes = 32
freqs = length // 2 + 1
freq_pad = 432
group = "ylo", "x", "yhi"
quad_rows = 72
shard_rows = 2 * rows + 2 * quad_rows
blocks = 16
f32 = jnp.float32
bf16 = jnp.bfloat16
nt = (((1,), (1,)), ((), ()))
tn = (((0,), (0,)), ((), ()))


def split_table(table):
    high = table.astype(ml_dtypes.bfloat16)
    low = (table - high.astype(np.float64)).astype(ml_dtypes.bfloat16)
    return high, low


@functools.cache
def dft_tables():
    freq = np.arange(freqs)
    angles = 2.0 * np.pi * ((freq[:, None] * np.arange(length)[None, :]) % length) / length
    forward = np.zeros((2, freq_pad, length))
    forward[0, :freqs] = np.cos(angles)
    forward[1, :freqs] = np.sin(angles)
    counts = np.where((freq == 0) | (freq == freqs - 1), 1.0, 2.0)[:, None] / math.sqrt(length)
    padded = np.zeros((2, freq_pad, length + edge))
    padded[0, :freqs, half : half + length] = np.cos(angles) * counts
    padded[1, :freqs, half : half + length] = np.sin(angles) * counts
    forward = forward.reshape(2 * freq_pad, length)
    padded = padded.reshape(2 * freq_pad, length + edge)
    bricks = length // cols
    backward = np.stack([padded[:, cols * j : cols * j + window] for j in range(bricks)])
    return split_table(forward) + split_table(backward)


def split(values):
    high = values.astype(bf16)
    low = (values - high.astype(f32)).astype(bf16)
    return high, low


def gather_kernel(template_ref, index_ref, out_ref, normed_ref):
    values = template_ref[...]
    centred = values - jnp.sum(values) / voxels
    normed_ref[...] = centred / jnp.sqrt(jnp.sum(centred * centred) + epsilon)
    index = index_ref[...]
    high = index >> 7
    low = index & 127

    def step(row, total):
        table = jnp.broadcast_to(normed_ref[pl.ds(row, 1), :], index.shape)
        found = jnp.take_along_axis(table, low, axis=1, mode="promise_in_bounds")
        return jnp.where(high == row, found, total)

    out_ref[...] = lax.fori_loop(0, voxels // 128, step, jnp.zeros(index.shape, f32))


def whiten_kernel(col_ref, rows_ref, fh_ref, fl_ref, bh_ref, bl_ref, voxels_ref, out_ref, x_ref):
    for plane in range(2):
        for j in range(length // cols):
            x_ref[rows * plane : rows * (plane + 1), cols * j : cols * (j + 1)] = rows_ref[
                plane * 8 + j
            ]
    xh, xl = split(x_ref[...])
    spec = (
        lax.dot_general(fh_ref[...], xh, nt, preferred_element_type=f32)
        + lax.dot_general(fh_ref[...], xl, nt, preferred_element_type=f32)
        + lax.dot_general(fl_ref[...], xh, nt, preferred_element_type=f32)
    )
    real = spec[:freq_pad]
    imag = spec[freq_pad:]
    power = real * real + imag * imag
    k = lax.broadcasted_iota(jnp.int32, power.shape, 0)
    before = jnp.where(k == 0, power[1:2], pltpu.roll(power, 1, 0))
    after = jnp.where(k == freqs - 1, power[freqs - 2 : freqs - 1], pltpu.roll(power, freq_pad - 1, 0))
    total = 2.0 * jnp.sum(power, axis=0, keepdims=True) - power[0:1] - power[freqs - 1 : freqs]
    smoothed = (before + power + after) / 3.0 + floor_share * (total / length) + epsilon
    weights = lax.rsqrt(smoothed)
    wh, wl = split(jnp.concatenate([real * weights, imag * weights], axis=0))
    out_ref[: 2 * rows, :] = (
        lax.dot_general(wh, bh_ref[0], tn, preferred_element_type=f32)
        + lax.dot_general(wl, bh_ref[0], tn, preferred_element_type=f32)
        + lax.dot_general(wh, bl_ref[0], tn, preferred_element_type=f32)
    )
    out_ref[2 * rows :, :] = voxels_ref[...]


def match_kernel(where_ref, g_ref, out_ref, v_ref, l_ref, w_ref, acc_ref, best_ref):
    plane0 = where_ref[0]
    core = where_ref[1]
    first = (core == 0).astype(f32)

    def load_plane(a, energy):
        plane = plane0 - half + a
        valid = jnp.logical_and(plane >= 0, plane < planes).astype(f32)
        plane = jnp.clip(plane, 0, planes - 1)
        z = plane % 16
        start = pl.multiple_of((plane // 16) * rows, rows)
        v_ref[a, half : half + rows, :] = g_ref[core, z, pl.ds(start, rows), :] * valid
        v_ref[a, 0:half, :] = g_ref[0, z, pl.ds(start, rows), :][rows - half :] * (valid * (1.0 - first))
        v_ref[a, half + rows : 56, :] = g_ref[1, z, pl.ds(start, rows), :][:half] * (valid * first)
        full = v_ref[a]
        v_ref[a] = pltpu.roll(full, (a % 4) * 32, 1)
        return energy + full * full

    energy = lax.fori_loop(0, edge, load_plane, jnp.zeros((56, window), f32))

    lane = lax.broadcasted_iota(jnp.int32, (blocks, window), 1)

    def expand(x, carry):
        at = pl.ds(pl.multiple_of(x * blocks, blocks), blocks)
        for quad in range(6):
            total = None
            for part in range(4):
                row = jnp.broadcast_to(v_ref[4 * quad + part, pl.ds(x, 1), :], (blocks, window))
                moved = pltpu.roll(row, 8, 1, stride=8, stride_axis=0)
                total = moved if total is None else jnp.where(lane >= 32 * part, moved, total)
            high, low = split(total)
            l_ref[at, window * quad : window * (quad + 1)] = high
            l_ref[at, 768 + window * quad : 768 + window * (quad + 1)] = low
            l_ref[at, 1536 + window * quad : 1536 + window * (quad + 1)] = high
        return carry

    lax.fori_loop(0, 56, expand, 0)

    def build(b, slot):
        for pair in range(planes // 2):
            for quad in range(6):
                moved = []
                for rot in (2 * pair, 2 * pair + 1):
                    at = 2 * rows + (rot // 16) * quad_rows + quad % 3 + 3 * b
                    row = g_ref[quad // 3, rot % 16, pl.ds(at, 1), :]
                    moved.append(pltpu.roll(jnp.broadcast_to(row, (8, window)), 0, 1, stride=1, stride_axis=0))
                high, low = split(jnp.concatenate(moved, axis=0))
                at = slice(16 * pair, 16 * pair + 16)
                w_ref[slot, at, window * quad : window * (quad + 1)] = high
                w_ref[slot, at, 768 + window * quad : 768 + window * (quad + 1)] = high
                w_ref[slot, at, 1536 + window * quad : 1536 + window * (quad + 1)] = low

    def product(b, slot):
        left = l_ref[pl.ds(pl.multiple_of(b * blocks, blocks), 32 * blocks), :]
        acc_ref[...] += lax.dot_general(left, w_ref[slot], nt, preferred_element_type=f32)

    acc_ref[...] = jnp.zeros_like(acc_ref)
    build(0, 0)

    def step(i, carry):
        build(2 * i + 1, 1)
        product(2 * i, 0)
        build(jnp.minimum(2 * i + 2, edge - 1), 0)
        product(2 * i + 1, 1)
        return carry

    lax.fori_loop(0, edge // 2, step, 0)

    best = jnp.maximum(acc_ref[:, :128], acc_ref[:, 128:])
    for shift in (64, 32, 16, 8):
        best = jnp.maximum(best, pltpu.roll(best, shift, 1))
    best_ref[...] = best
    lanes = lax.broadcasted_iota(jnp.int32, (rows, window), 1)
    score = jnp.zeros((rows, window), f32)
    for block in range(13):
        score = jnp.where(lanes // 8 == block, best_ref[pl.ds(blocks - 1 - block, rows, stride=blocks), :], score)

    def shifted(values, count):
        return pltpu.roll(values, values.shape[0] - count, 0)

    sums = energy
    for count in (1, 2, 4):
        sums = sums + shifted(sums, count)
    sums = sums + shifted(sums, 8) + shifted(sums, 16)
    sums = sums[:rows]
    for count in (1, 2, 4):
        sums = sums + pltpu.roll(sums, window - count, 1)
    sums = sums + pltpu.roll(sums, window - 8, 1) + pltpu.roll(sums, window - 16, 1)
    out_ref[...] = (score * lax.rsqrt(sums / voxels + epsilon))[:, :cols]


def shards(volume, template, voxel_maps):
    ylo, z, core = lax.axis_index("ylo"), lax.axis_index("z"), lax.axis_index("core")
    column = lax.axis_index("x") * 2 + lax.axis_index("yhi")
    vmem = pl.BlockSpec(memory_space=pltpu.VMEM)
    smem = pl.BlockSpec(memory_space=pltpu.SMEM)

    copies = jnp.broadcast_to(volume, (16, rows, cols))
    full_rows = lax.all_to_all(copies, group, split_axis=0, concat_axis=0, tiled=True)

    maps = voxel_maps.reshape(2, half, edge, edge)
    maps = jnp.pad(maps, ((0, 0), (0, 0), (0, 0), (0, 8)), constant_values=-1)
    maps = maps.transpose(0, 2, 1, 3).reshape(2, quad_rows, 128)
    own = lax.dynamic_index_in_dim(maps, core, 0, keepdims=False)
    other = lax.ppermute(own, "ylo", [(0, 1), (1, 0)])
    index = jnp.concatenate([jnp.where(ylo == 0, own, other), jnp.where(ylo == 0, other, own)])
    rotated = pl.pallas_call(
        gather_kernel,
        out_shape=jax.ShapeDtypeStruct((2 * quad_rows, 128), f32),
        in_specs=[vmem, vmem],
        out_specs=vmem,
        scratch_shapes=[pltpu.VMEM((voxels // 128, 128), f32)],
        name="rotate",
    )(template.reshape(voxels // 128, 128), index)

    tables = [jnp.asarray(table) for table in dft_tables()]
    shard = pl.pallas_call(
        whiten_kernel,
        out_shape=jax.ShapeDtypeStruct((shard_rows, 128), f32),
        grid_spec=pltpu.PrefetchScalarGridSpec(
            num_scalar_prefetch=1,
            grid=(1,),
            in_specs=[
                pl.BlockSpec((16, rows, cols), lambda i, c: (0, 0, 0)),
                pl.BlockSpec((2 * freq_pad, length), lambda i, c: (0, 0)),
                pl.BlockSpec((2 * freq_pad, length), lambda i, c: (0, 0)),
                pl.BlockSpec((1, 2 * freq_pad, window), lambda i, c: (c[0], 0, 0)),
                pl.BlockSpec((1, 2 * freq_pad, window), lambda i, c: (c[0], 0, 0)),
                pl.BlockSpec((2 * quad_rows, 128), lambda i, c: (0, 0)),
            ],
            out_specs=pl.BlockSpec((shard_rows, 128), lambda i, c: (0, 0)),
            scratch_shapes=[pltpu.VMEM((2 * rows, length), f32)],
        ),
        compiler_params=pltpu.CompilerParams(vmem_limit_bytes=32 * 2**20),
        name="whiten",
    )(column[None].astype(jnp.int32), full_rows, *tables, rotated)

    gathered = lax.all_gather(shard, "z", axis=0, tiled=True)
    gathered = lax.all_gather(gathered, "core", axis=0, tiled=True)
    place = jnp.stack([ylo * 16 + z, core]).astype(jnp.int32)
    best = pl.pallas_call(
        match_kernel,
        out_shape=jax.ShapeDtypeStruct((rows, cols), f32),
        in_specs=[smem, vmem],
        out_specs=vmem,
        scratch_shapes=[
            pltpu.VMEM((edge, 56, window), f32),
            pltpu.VMEM((56 * blocks, 2304), bf16),
            pltpu.VMEM((2, 256, 2304), bf16),
            pltpu.VMEM((32 * blocks, 256), f32),
            pltpu.VMEM((32 * blocks, 128), f32),
        ],
        compiler_params=pltpu.CompilerParams(vmem_limit_bytes=48 * 2**20),
        name="match",
    )(place, gathered.reshape(2, 16, shard_rows, 128))
    return best[None]


def solution(mesh):
    inner = Mesh(mesh.devices.reshape(2, 16, 2, 4, 2), ("ylo", "z", "core", "x", "yhi"))
    orient, bricks = ("ylo", "z"), ("x", "yhi")
    return jax.shard_map(
        shards,
        mesh=inner,
        in_specs=(P(orient, "core", bricks), P(), P(orient, None)),
        out_specs=P(orient, "core", bricks),
        check_vma=False,
    )
```

```python
import functools
import math

import jax
import jax.numpy as jnp
import ml_dtypes
import numpy as np
from jax import lax
from jax.experimental import pallas as pl
from jax.experimental.pallas import tpu as pltpu
from jax.sharding import Mesh
from jax.sharding import PartitionSpec as P

epsilon = 1e-06
floor_share = 0.1
edge = 24
half = 12
voxels = edge**3
length = 832
cols = 104
window = 128
rows = 32
planes = 32
freqs = length // 2 + 1
freq_pad = 432
group = "ylo", "x", "yhi"
half_rows = 60
shard_rows = 2 * rows + half_rows
span = planes // 2 + edge
rots = 16
blocks = 16
depth = 32 * edge
f32 = jnp.float32
bf16 = jnp.bfloat16
nt = (((1,), (1,)), ((), ()))
tn = (((0,), (0,)), ((), ()))


def split_table(table):
    high = table.astype(ml_dtypes.bfloat16)
    low = (table - high.astype(np.float64)).astype(ml_dtypes.bfloat16)
    return high, low


@functools.cache
def dft_tables():
    freq = np.arange(freqs)
    angles = 2.0 * np.pi * ((freq[:, None] * np.arange(length)[None, :]) % length) / length
    forward = np.zeros((2, freq_pad, length))
    forward[0, :freqs] = np.cos(angles)
    forward[1, :freqs] = np.sin(angles)
    counts = np.where((freq == 0) | (freq == freqs - 1), 1.0, 2.0)[:, None] / math.sqrt(length)
    padded = np.zeros((2, freq_pad, length + edge))
    padded[0, :freqs, half : half + length] = np.cos(angles) * counts
    padded[1, :freqs, half : half + length] = np.sin(angles) * counts
    forward = forward.reshape(2 * freq_pad, length)
    padded = padded.reshape(2 * freq_pad, length + edge)
    bricks = length // cols
    backward = np.stack([padded[:, cols * j : cols * j + window] for j in range(bricks)])
    return split_table(forward) + split_table(backward)


def split(values):
    high = values.astype(bf16)
    low = (values - high.astype(f32)).astype(bf16)
    return high, low


def rotate_kernel(core_ref, template_ref, map_ref, out_ref, normed_ref, index_ref):
    values = template_ref[...]
    centred = values - jnp.sum(values) / voxels
    normed = centred / jnp.sqrt(jnp.sum(centred * centred) + epsilon)
    normed_ref[...] = jnp.zeros_like(normed_ref)
    for a in range(edge):
        at = slice(edge * (a // 5), edge * (a // 5 + 1))
        normed_ref[at, edge * (a % 5) : edge * (a % 5 + 1)] = normed[a]
    index_ref[...] = jnp.full_like(index_ref, -1)

    for core in range(2):

        @pl.when(core_ref[0] == core)
        def place():
            for a in range(edge):
                for b in range(half):
                    start = (a * edge + half * core + b) * edge
                    at = half * (a // 5) + b
                    index_ref[at : at + 1, edge * (a % 5) : edge * (a % 5 + 1)] = map_ref[
                        0:1, start : start + edge
                    ]

    def gather(i, carry):
        at = pl.ds(pl.multiple_of(8 * i, 8), 8)
        index = index_ref[at, :]
        source = jnp.maximum(index, 0)
        a = source // (edge * edge)
        rest = source - a * (edge * edge)
        b = rest // edge
        c = rest - b * edge
        group = a // 5
        lane = (a - 5 * group) * edge + c
        high = jnp.where(index < 0, -1, group * edge + b)
        totals = [jnp.zeros((8, 128), f32) for _ in range(4)]
        for row in range(5 * edge):
            table = jnp.broadcast_to(normed_ref[row : row + 1, :], (8, 128))
            found = jnp.take_along_axis(table, lane, axis=1, mode="promise_in_bounds")
            totals[row % 4] = jnp.where(high == row, found, totals[row % 4])
        out_ref[at, :] = (totals[0] + totals[1]) + (totals[2] + totals[3])
        return carry

    lax.fori_loop(0, 8, gather, 0, unroll=2)


def whiten_kernel(
    place_ref, rows_ref, fh_hbm, fl_hbm, bh_hbm, bl_hbm, own_ref, out_ref, x_ref, fh_ref, fl_ref, bh_ref, bl_ref, sems
):
    column = place_ref[0]
    copies = [
        pltpu.make_async_copy(fh_hbm, fh_ref, sems.at[0]),
        pltpu.make_async_copy(fl_hbm, fl_ref, sems.at[1]),
        pltpu.make_async_copy(bh_hbm.at[column], bh_ref, sems.at[2]),
        pltpu.make_async_copy(bl_hbm.at[column], bl_ref, sems.at[3]),
    ]
    for copy in copies:
        copy.start()
    out_ref[0, 2 * rows :, :] = own_ref[:half_rows, :]
    for plane in range(2):
        for j in range(length // cols):
            x_ref[rows * plane : rows * (plane + 1), cols * j : cols * (j + 1)] = rows_ref[
                plane * 8 + j
            ]
    xh, xl = split(x_ref[...])
    copies[0].wait()
    spec = lax.dot_general(fh_ref[...], xh, nt, preferred_element_type=f32) + lax.dot_general(
        fh_ref[...], xl, nt, preferred_element_type=f32
    )
    copies[1].wait()
    spec = spec + lax.dot_general(fl_ref[...], xh, nt, preferred_element_type=f32)
    real = spec[:freq_pad]
    imag = spec[freq_pad:]
    power = real * real + imag * imag
    k = lax.broadcasted_iota(jnp.int32, power.shape, 0)
    before = jnp.where(k == 0, power[1:2], pltpu.roll(power, 1, 0))
    after = jnp.where(k == freqs - 1, power[freqs - 2 : freqs - 1], pltpu.roll(power, freq_pad - 1, 0))
    total = 2.0 * jnp.sum(power, axis=0, keepdims=True) - power[0:1] - power[freqs - 1 : freqs]
    smoothed = (before + power + after) / 3.0 + floor_share * (total / length) + epsilon
    weights = lax.rsqrt(smoothed)
    wh, wl = split(jnp.concatenate([real * weights, imag * weights], axis=0))
    copies[2].wait()
    copies[3].wait()
    out_ref[0, : 2 * rows, :] = (
        lax.dot_general(wh, bh_ref[...], tn, preferred_element_type=f32)
        + lax.dot_general(wl, bh_ref[...], tn, preferred_element_type=f32)
        + lax.dot_general(wh, bl_ref[...], tn, preferred_element_type=f32)
    )


def match_kernel(
    where_ref, own_hbm, other_hbm, mine_ref, theirs_ref, scale_ref, g_ref, v_ref, t_ref, l_ref, w_ref, acc_ref, best_ref, score_ref, sems
):
    z0 = where_ref[0]
    ylo = where_ref[1]
    core = where_ref[2]
    first = (core == 0).astype(f32)
    copies = [
        pltpu.make_async_copy(own_hbm, g_ref.at[core], sems.at[0]),
        pltpu.make_async_copy(other_hbm, g_ref.at[1 - core], sems.at[1]),
    ]
    for copy in copies:
        copy.start()
    for copy in copies:
        copy.wait()

    def load_plane(j, energy):
        plane = z0 - half + j
        valid = jnp.logical_and(plane >= 0, plane < planes).astype(f32)
        plane = jnp.clip(plane, 0, planes - 1)
        z = plane % 16
        start = pl.multiple_of((plane // 16) * rows, rows)
        v_ref[j, half : half + rows, :] = g_ref[core, z, pl.ds(start, rows), :] * valid
        v_ref[j, 0:half, :] = g_ref[0, z, pl.ds(start, rows), :][rows - half :] * (valid * (1.0 - first))
        v_ref[j, half + rows : 56, :] = g_ref[1, z, pl.ds(start, rows), :][:half] * (valid * first)
        full = v_ref[j]
        v_ref[j] = pltpu.roll(full, (j % 4) * 32, 1)
        inside = jnp.logical_and(j >= 16 * ylo, j < 16 * ylo + edge).astype(f32)
        return energy + full * full * inside

    energy = lax.fori_loop(0, span, load_plane, jnp.zeros((56, window), f32), unroll=4)

    lane = lax.broadcasted_iota(jnp.int32, (blocks, window), 1)
    cell = lax.broadcasted_iota(jnp.int32, (half, window), 1)

    t_ref[...] = jnp.zeros_like(t_ref)

    def widen(r, carry):
        for core_half in range(2):
            for quad in range(6):
                total = jnp.zeros((half, window), f32)
                for part in range(4):
                    a = 4 * quad + part
                    at = 2 * rows + half * (a // 5)
                    source = g_ref[core_half, r, at : at + half, :]
                    moved = pltpu.roll(source, (32 * part - edge * (a % 5)) % window, 1)
                    keep = jnp.logical_and(cell >= 32 * part, cell < 32 * part + edge)
                    total = jnp.where(keep, moved, total)
                t_ref[r, quad, 1 + half * core_half : 1 + half * (core_half + 1), :] = total
        return carry

    lax.fori_loop(0, rots, widen, 0, unroll=2)

    def expand(u, carry):
        here = pl.ds(pl.multiple_of(u * blocks, blocks), blocks)
        for parity in range(2):
            for quad in range(span // 4):
                total = None
                for part in range(4):
                    row = jnp.broadcast_to(v_ref[4 * quad + part, pl.ds(2 * u + parity, 1), :], (blocks, window))
                    moved = pltpu.roll(row, 8, 1, stride=8, stride_axis=0)
                    total = moved if total is None else jnp.where(lane >= 32 * part, moved, total)
                high, low = split(total)
                for k, piece in enumerate((high, low, high)):
                    at = window * (6 * quad + 3 * parity + k)
                    l_ref[here, at : at + window] = piece
        return carry

    lax.fori_loop(0, 28, expand, 0, unroll=2)

    def build(v, slot):
        for tap, targets in ((-1, ((0, 1),)), (0, ((0, 0), (1, 1))), (1, ((1, 0),))):
            for pair in range(rots // 2):
                for quad in range(6):
                    moved = []
                    for r in (2 * pair, 2 * pair + 1):
                        row = t_ref[r, quad, pl.ds(2 * v + tap + 1, 1), :]
                        moved.append(pltpu.roll(jnp.broadcast_to(row, (8, window)), 0, 1, stride=1, stride_axis=0))
                    high, low = split(jnp.concatenate(moved, axis=0))
                    for parity, p in targets:
                        for k, piece in enumerate((high, high, low)):
                            at = window * (6 * quad + 3 * parity + k)
                            place = 128 * p + 16 * pair
                            w_ref[slot, place : place + 16, at : at + window] = piece

    def product(v, slot):
        here = pl.ds(pl.multiple_of(v * blocks, blocks), 16 * blocks)
        left = jnp.concatenate([l_ref[here, : 6 * depth], l_ref[here, 4 * depth : 10 * depth]], axis=0)
        acc_ref[...] += lax.dot_general(left, w_ref[slot], nt, preferred_element_type=f32)

    acc_ref[...] = jnp.zeros_like(acc_ref)
    build(0, 0)

    def step(i, carry):
        build(2 * i + 1, 1)
        product(2 * i, 0)
        build(2 * i + 2, 0)
        product(2 * i + 1, 1)
        return carry

    lax.fori_loop(0, 6, step, 0)
    product(12, 0)

    lanes = lax.broadcasted_iota(jnp.int32, (16, window), 1)
    for p in range(2):
        best = acc_ref[:, 128 * p : 128 * (p + 1)]
        for shift in (64, 32, 16, 8):
            best = jnp.maximum(best, pltpu.roll(best, shift, 1))
        best_ref[...] = best
        for plane in range(2):
            score = jnp.zeros((16, window), f32)
            for block in range(13):
                found = best_ref[pl.ds(256 * plane + blocks - 1 - block, 16, stride=blocks), :]
                score = jnp.where(lanes // 8 == block, found, score)
            score_ref[pl.ds(rows * plane + p, 16, stride=2), :] = score
    mine_ref[...] = score_ref[pl.ds(pl.multiple_of(rows * ylo, rows), rows), :][:, :cols]
    theirs_ref[...] = score_ref[pl.ds(pl.multiple_of(rows * (1 - ylo), rows), rows), :][:, :cols]

    def shifted(values, count):
        return pltpu.roll(values, values.shape[0] - count, 0)

    sums = energy
    for count in (1, 2, 4):
        sums = sums + shifted(sums, count)
    sums = sums + shifted(sums, 8) + shifted(sums, 16)
    sums = sums[:rows]
    for count in (1, 2, 4):
        sums = sums + pltpu.roll(sums, window - count, 1)
    sums = sums + pltpu.roll(sums, window - 8, 1) + pltpu.roll(sums, window - 16, 1)
    scale_ref[...] = lax.rsqrt(sums / voxels + epsilon)[:, :cols]


def match_scratch():
    return [
        pltpu.VMEM((2, 16, shard_rows, 128), f32),
        pltpu.VMEM((span, 56, window), f32),
        pltpu.VMEM((rots, 6, 32, window), f32),
        pltpu.VMEM((28 * blocks, 10 * depth), bf16),
        pltpu.VMEM((2, 256, 6 * depth), bf16),
        pltpu.VMEM((32 * blocks, 256), f32),
        pltpu.VMEM((32 * blocks, 128), f32),
        pltpu.VMEM((2 * rows, 128), f32),
        pltpu.SemaphoreType.DMA((2,)),
    ]


def shards(volume, template, voxel_maps):
    ylo, z, core = lax.axis_index("ylo"), lax.axis_index("z"), lax.axis_index("core")
    column = lax.axis_index("x") * 2 + lax.axis_index("yhi")
    vmem = pl.BlockSpec(memory_space=pltpu.VMEM)
    hbm = pl.BlockSpec(memory_space=pl.ANY)
    smem = pl.BlockSpec(memory_space=pltpu.SMEM)

    copies = jnp.broadcast_to(volume, (16, rows, cols))
    full_rows = lax.all_to_all(copies, group, split_axis=0, concat_axis=0, tiled=True)

    own = pl.pallas_call(
        rotate_kernel,
        out_shape=jax.ShapeDtypeStruct((64, 128), f32),
        grid_spec=pltpu.PrefetchScalarGridSpec(
            num_scalar_prefetch=1,
            grid=(1,),
            in_specs=[
                pl.BlockSpec((edge, edge, edge), lambda i, c: (0, 0, 0)),
                pl.BlockSpec((1, voxels), lambda i, c: (0, 0)),
            ],
            out_specs=pl.BlockSpec((64, 128), lambda i, c: (0, 0)),
            scratch_shapes=[pltpu.VMEM((5 * edge, 128), f32), pltpu.VMEM((64, 128), jnp.int32)],
        ),
        name="rotate",
    )(core[None].astype(jnp.int32), template, voxel_maps)

    tables = [jnp.asarray(table) for table in dft_tables()]
    shard = pl.pallas_call(
        whiten_kernel,
        out_shape=jax.ShapeDtypeStruct((1, shard_rows, 128), f32),
        grid_spec=pltpu.PrefetchScalarGridSpec(
            num_scalar_prefetch=1,
            grid=(1,),
            in_specs=[
                pl.BlockSpec((16, rows, cols), lambda i, c: (0, 0, 0)),
                hbm,
                hbm,
                hbm,
                hbm,
                pl.BlockSpec((64, 128), lambda i, c: (0, 0)),
            ],
            out_specs=pl.BlockSpec((1, shard_rows, 128), lambda i, c: (0, 0, 0)),
            scratch_shapes=[
                pltpu.VMEM((2 * rows, length), f32),
                pltpu.VMEM((2 * freq_pad, length), bf16),
                pltpu.VMEM((2 * freq_pad, length), bf16),
                pltpu.VMEM((2 * freq_pad, window), bf16),
                pltpu.VMEM((2 * freq_pad, window), bf16),
                pltpu.SemaphoreType.DMA((4,)),
            ],
        ),
        compiler_params=pltpu.CompilerParams(vmem_limit_bytes=60 * 2**20),
        name="whiten",
    )(column[None].astype(jnp.int32), full_rows, *tables, own)

    gathered = lax.all_gather(shard, "z", axis=0, tiled=True)
    partner = lax.ppermute(gathered, "core", [(0, 1), (1, 0)])
    place = jnp.stack([z, ylo, core]).astype(jnp.int32)
    mine, theirs, scale = pl.pallas_call(
        match_kernel,
        out_shape=[jax.ShapeDtypeStruct((rows, cols), f32)] * 3,
        in_specs=[smem, hbm, hbm],
        out_specs=[vmem] * 3,
        scratch_shapes=match_scratch(),
        compiler_params=pltpu.CompilerParams(vmem_limit_bytes=56 * 2**20),
        name="match",
    )(place, gathered, partner)
    received = lax.ppermute(theirs, "ylo", [(0, 1), (1, 0)])
    return (jnp.maximum(mine, received) * scale)[None]


def solution(mesh):
    inner = Mesh(mesh.devices.reshape(2, 16, 2, 4, 2), ("ylo", "z", "core", "x", "yhi"))
    orient, bricks = ("ylo", "z"), ("x", "yhi")
    return jax.shard_map(
        shards,
        mesh=inner,
        in_specs=(P(orient, "core", bricks), P(), P(orient, None)),
        out_specs=P(orient, "core", bricks),
        check_vma=False,
    )
```

```python
import functools
import math

import jax
import jax.numpy as jnp
import ml_dtypes
import numpy as np
from jax import lax
from jax.experimental import pallas as pl
from jax.experimental.pallas import tpu as pltpu
from jax.sharding import Mesh
from jax.sharding import PartitionSpec as P

epsilon = 1e-06
floor_share = 0.1
edge = 24
half = 12
voxels = edge**3
length = 832
cols = 104
window = 128
rows = 32
planes = 32
freqs = length // 2 + 1
freq_pad = 432
group = "ylo", "x", "yhi"
half_rows = 56
shard_rows = 2 * rows + half_rows
span = planes // 2 + edge
rots = 16
blocks = 16
depth = 32 * edge
f32 = jnp.float32
bf16 = jnp.bfloat16
nt = (((1,), (1,)), ((), ()))
tn = (((0,), (0,)), ((), ()))


def split_table(table):
    high = table.astype(ml_dtypes.bfloat16)
    low = (table - high.astype(np.float64)).astype(ml_dtypes.bfloat16)
    return high, low


@functools.cache
def dft_tables():
    freq = np.arange(freqs)
    angles = 2.0 * np.pi * ((freq[:, None] * np.arange(length)[None, :]) % length) / length
    forward = np.zeros((2, freq_pad, length))
    forward[0, :freqs] = np.cos(angles)
    forward[1, :freqs] = np.sin(angles)
    counts = np.where((freq == 0) | (freq == freqs - 1), 1.0, 2.0)[:, None] / math.sqrt(length)
    padded = np.zeros((2, freq_pad, length + edge))
    padded[0, :freqs, half : half + length] = np.cos(angles) * counts
    padded[1, :freqs, half : half + length] = np.sin(angles) * counts
    forward = forward.reshape(2 * freq_pad, length)
    padded = padded.reshape(2 * freq_pad, length + edge)
    bricks = length // cols
    backward = np.stack([padded[:, cols * j : cols * j + window] for j in range(bricks)])
    return np.stack(split_table(forward)), np.stack(split_table(backward))


def split(values):
    high = values.astype(bf16)
    low = (values - high.astype(f32)).astype(bf16)
    return high, low


def cells_of(a, b):
    if a < 20:
        return [(half * (a // 5) + b, edge * (a % 5), 0, edge)]
    if b < 8:
        return [(48 + b, edge * (a - 20), 0, edge)]
    if a < 22:
        return [(48 + 4 * (a - 20) + b - 8, 96, 0, edge)]
    return [(half * j + b - 4 * (a - 22), 120, 8 * j, 8) for j in range(3)]


def rotate_kernel(core_ref, template_ref, map_ref, out_ref, normed_ref, index_ref):
    values = template_ref[...]
    centred = values - jnp.sum(values) / voxels
    normed = centred / jnp.sqrt(jnp.sum(centred * centred) + epsilon)
    normed_ref[...] = jnp.zeros_like(normed_ref)
    for a in range(edge):
        at = slice(edge * (a // 5), edge * (a // 5 + 1))
        normed_ref[at, edge * (a % 5) : edge * (a % 5 + 1)] = normed[a]
    index_ref[...] = jnp.full_like(index_ref, -1)

    for core in range(2):

        @pl.when(core_ref[0] == core)
        def place():
            for a in range(edge):
                for b in range(half):
                    start = (a * edge + half * core + b) * edge
                    for at, lane, first, width in cells_of(a, b):
                        index_ref[at : at + 1, lane : lane + width] = map_ref[
                            0:1, start + first : start + first + width
                        ]

    def gather(i, carry):
        at = pl.ds(pl.multiple_of(8 * i, 8), 8)
        index = index_ref[at, :]
        source = jnp.maximum(index, 0)
        a = source // (edge * edge)
        rest = source - a * (edge * edge)
        b = rest // edge
        c = rest - b * edge
        group = a // 5
        lane = (a - 5 * group) * edge + c
        high = jnp.where(index < 0, -1, group * edge + b)
        totals = [jnp.zeros((8, 128), f32) for _ in range(4)]
        for row in range(5 * edge):
            table = jnp.broadcast_to(normed_ref[row : row + 1, :], (8, 128))
            found = jnp.take_along_axis(table, lane, axis=1, mode="promise_in_bounds")
            totals[row % 4] = jnp.where(high == row, found, totals[row % 4])
        out_ref[at, :] = (totals[0] + totals[1]) + (totals[2] + totals[3])
        return carry

    lax.fori_loop(0, half_rows // 8, gather, 0, unroll=7)


def whiten_kernel(
    place_ref, rows_ref, f_hbm, b_hbm, own_ref, out_ref, x_ref, fh_ref, fl_ref, bh_ref, bl_ref, sems
):
    column = place_ref[0]
    copies = [
        pltpu.make_async_copy(f_hbm.at[0], fh_ref, sems.at[0]),
        pltpu.make_async_copy(f_hbm.at[1], fl_ref, sems.at[1]),
        pltpu.make_async_copy(b_hbm.at[0, column], bh_ref, sems.at[2]),
        pltpu.make_async_copy(b_hbm.at[1, column], bl_ref, sems.at[3]),
    ]
    for copy in copies:
        copy.start()
    out_ref[0, 2 * rows :, :] = own_ref[...]
    for plane in range(2):
        for j in range(length // cols):
            x_ref[rows * plane : rows * (plane + 1), cols * j : cols * (j + 1)] = rows_ref[
                plane * 8 + j
            ]
    xh, xl = split(x_ref[...])
    copies[0].wait()
    spec = lax.dot_general(fh_ref[...], xh, nt, preferred_element_type=f32) + lax.dot_general(
        fh_ref[...], xl, nt, preferred_element_type=f32
    )
    copies[1].wait()
    spec = spec + lax.dot_general(fl_ref[...], xh, nt, preferred_element_type=f32)
    real = spec[:freq_pad]
    imag = spec[freq_pad:]
    power = real * real + imag * imag
    k = lax.broadcasted_iota(jnp.int32, power.shape, 0)
    before = jnp.where(k == 0, power[1:2], pltpu.roll(power, 1, 0))
    after = jnp.where(k == freqs - 1, power[freqs - 2 : freqs - 1], pltpu.roll(power, freq_pad - 1, 0))
    total = 2.0 * jnp.sum(power, axis=0, keepdims=True) - power[0:1] - power[freqs - 1 : freqs]
    smoothed = (before + power + after) / 3.0 + floor_share * (total / length) + epsilon
    weights = lax.rsqrt(smoothed)
    wh, wl = split(jnp.concatenate([real * weights, imag * weights], axis=0))
    copies[2].wait()
    copies[3].wait()
    out_ref[0, : 2 * rows, :] = (
        lax.dot_general(wh, bh_ref[...], tn, preferred_element_type=f32)
        + lax.dot_general(wl, bh_ref[...], tn, preferred_element_type=f32)
        + lax.dot_general(wh, bl_ref[...], tn, preferred_element_type=f32)
    )


def match_kernel(
    where_ref, own_ref, other_ref, mine_ref, theirs_ref, scale_ref, v_ref, t_ref, l_ref, w_ref, acc_ref, best_ref, score_ref
):
    z0 = where_ref[0]
    ylo = where_ref[1]
    core = where_ref[2]
    first = (core == 0).astype(f32)

    def load_plane(j, energy):
        plane = z0 - half + j
        valid = jnp.logical_and(plane >= 0, plane < planes).astype(f32)
        plane = jnp.clip(plane, 0, planes - 1)
        z = plane % 16
        start = pl.multiple_of((plane // 16) * rows, rows)
        near = other_ref[z, pl.ds(start, rows), :]
        v_ref[j, half : half + rows, :] = own_ref[z, pl.ds(start, rows), :] * valid
        v_ref[j, 0:half, :] = near[rows - half :] * (valid * (1.0 - first))
        v_ref[j, half + rows : 56, :] = near[:half] * (valid * first)
        full = v_ref[j]
        v_ref[j] = pltpu.roll(full, (j % 4) * 32, 1)
        inside = jnp.logical_and(j >= 16 * ylo, j < 16 * ylo + edge).astype(f32)
        return energy + full * full * inside

    energy = lax.fori_loop(0, span, load_plane, jnp.zeros((56, window), f32), unroll=4)

    lane = lax.broadcasted_iota(jnp.int32, (blocks, window), 1)
    place = lax.broadcasted_iota(jnp.int32, (blocks, window), 0)
    owner = ((lane + 8 * place + 8) & (window - 1)) // 32
    cell = lax.broadcasted_iota(jnp.int32, (half, window), 1)

    t_ref[...] = jnp.zeros_like(t_ref)

    def widen(sources):
        def placed(total, source, lane_from, lane_to, width):
            moved = pltpu.roll(source, (lane_to - lane_from) % window, 1)
            at = cell[: source.shape[0]]
            return jnp.where(jnp.logical_and(at >= lane_to, at < lane_to + width), moved, total)

        def step(r, carry):
            for k, source_ref in enumerate(sources):
                put = 1 + half * k
                for quad in range(6):
                    for low, high in ((0, 8), (8, half)) if quad == 5 else ((0, half),):
                        total = jnp.zeros((high - low, window), f32)
                        for part in range(4):
                            for at, lane_from, c, width in cells_of(4 * quad + part, low):
                                at = 2 * rows + at
                                source = source_ref[r, at : at + high - low, :]
                                total = placed(total, source, lane_from, 32 * part + c, width)
                        t_ref[r, quad, put + low : put + high, :] = total
            return carry

        lax.fori_loop(0, rots, step, 0, unroll=2)

    @pl.when(core == 0)
    def from_first():
        widen((own_ref, other_ref))

    @pl.when(core != 0)
    def from_second():
        widen((other_ref, own_ref))

    def expand(u, carry):
        here = pl.ds(pl.multiple_of(u * blocks, blocks), blocks)
        for parity in range(2):
            for quad in range(span // 4):
                total = None
                for part in range(4):
                    row = jnp.broadcast_to(v_ref[4 * quad + part, pl.ds(2 * u + parity, 1), :], (blocks, window))
                    total = row if total is None else jnp.where(owner >= part, row, total)
                total = pltpu.roll(total, 8, 1, stride=8, stride_axis=0)
                high, low = split(total)
                for k, piece in enumerate((high, low, high)):
                    at = window * (6 * quad + 3 * parity + k)
                    l_ref[here, at : at + window] = piece
        return carry

    lax.fori_loop(0, 28, expand, 0, unroll=4)

    def build(v, slot):
        for tap, targets in ((-1, ((0, 1),)), (0, ((0, 0), (1, 1))), (1, ((1, 0),))):
            for pair in range(rots // 2):
                for quad in range(6):
                    moved = []
                    for r in (2 * pair, 2 * pair + 1):
                        row = t_ref[r, quad, pl.ds(2 * v + tap + 1, 1), :]
                        moved.append(pltpu.roll(jnp.broadcast_to(row, (8, window)), 0, 1, stride=1, stride_axis=0))
                    high, low = split(jnp.concatenate(moved, axis=0))
                    for parity, p in targets:
                        for k, piece in enumerate((high, high, low)):
                            at = window * (6 * quad + 3 * parity + k)
                            place = 128 * p + 16 * pair
                            w_ref[slot, place : place + 16, at : at + window] = piece

    def product(v, slot):
        here = pl.ds(pl.multiple_of(v * blocks, blocks), 16 * blocks)
        left = jnp.concatenate([l_ref[here, : 6 * depth], l_ref[here, 4 * depth : 10 * depth]], axis=0)
        acc_ref[...] += lax.dot_general(left, w_ref[slot], nt, preferred_element_type=f32)

    acc_ref[...] = jnp.zeros_like(acc_ref)
    build(0, 0)

    def step(i, carry):
        build(2 * i + 1, 1)
        product(2 * i, 0)
        build(2 * i + 2, 0)
        product(2 * i + 1, 1)
        return carry

    lax.fori_loop(0, 6, step, 0)
    product(12, 0)

    lanes = lax.broadcasted_iota(jnp.int32, (16, window), 1)
    for p in range(2):
        best = acc_ref[:, 128 * p : 128 * (p + 1)]
        for shift in (64, 32, 16, 8):
            best = jnp.maximum(best, pltpu.roll(best, shift, 1))
        best_ref[...] = best
        for plane in range(2):
            score = jnp.zeros((16, window), f32)
            for block in range(13):
                found = best_ref[pl.ds(256 * plane + blocks - 1 - block, 16, stride=blocks), :]
                score = jnp.where(lanes // 8 == block, found, score)
            score_ref[pl.ds(rows * plane + p, 16, stride=2), :] = score
    mine_ref[...] = score_ref[pl.ds(pl.multiple_of(rows * ylo, rows), rows), :][:, :cols]
    theirs_ref[...] = score_ref[pl.ds(pl.multiple_of(rows * (1 - ylo), rows), rows), :][:, :cols]

    def shifted(values, count):
        return pltpu.roll(values, values.shape[0] - count, 0)

    sums = energy
    for count in (1, 2, 4):
        sums = sums + shifted(sums, count)
    sums = sums + shifted(sums, 8) + shifted(sums, 16)
    sums = sums[:rows]
    for count in (1, 2, 4):
        sums = sums + pltpu.roll(sums, window - count, 1)
    sums = sums + pltpu.roll(sums, window - 8, 1) + pltpu.roll(sums, window - 16, 1)
    scale_ref[...] = lax.rsqrt(sums / voxels + epsilon)[:, :cols]


def match_scratch():
    return [
        pltpu.VMEM((span, 56, window), f32),
        pltpu.VMEM((rots, 6, 32, window), f32),
        pltpu.VMEM((28 * blocks, 10 * depth), bf16),
        pltpu.VMEM((2, 256, 6 * depth), bf16),
        pltpu.VMEM((32 * blocks, 256), f32),
        pltpu.VMEM((32 * blocks, 128), f32),
        pltpu.VMEM((2 * rows, 128), f32),
    ]


def shards(volume, template, voxel_maps):
    ylo, z, core = lax.axis_index("ylo"), lax.axis_index("z"), lax.axis_index("core")
    column = lax.axis_index("x") * 2 + lax.axis_index("yhi")
    vmem = pl.BlockSpec(memory_space=pltpu.VMEM)
    hbm = pl.BlockSpec(memory_space=pltpu.HBM)
    smem = pl.BlockSpec(memory_space=pltpu.SMEM)

    copies = jnp.broadcast_to(volume, (16, rows, cols))
    full_rows = lax.all_to_all(copies, group, split_axis=0, concat_axis=0, tiled=True)

    own = pl.pallas_call(
        rotate_kernel,
        out_shape=jax.ShapeDtypeStruct((half_rows, 128), f32),
        in_specs=[smem, vmem, vmem],
        out_specs=vmem,
        scratch_shapes=[pltpu.VMEM((5 * edge, 128), f32), pltpu.VMEM((half_rows, 128), jnp.int32)],
        compiler_params=pltpu.CompilerParams(vmem_limit_bytes=8 * 2**20),
        name="rotate",
    )(core[None].astype(jnp.int32), template, voxel_maps)

    tables = [jnp.asarray(table) for table in dft_tables()]
    shard = pl.pallas_call(
        whiten_kernel,
        out_shape=jax.ShapeDtypeStruct((1, shard_rows, 128), f32),
        in_specs=[smem, vmem, hbm, hbm, vmem],
        out_specs=vmem,
        scratch_shapes=[
            pltpu.VMEM((2 * rows, length), f32),
            pltpu.VMEM((2 * freq_pad, length), bf16),
            pltpu.VMEM((2 * freq_pad, length), bf16),
            pltpu.VMEM((2 * freq_pad, window), bf16),
            pltpu.VMEM((2 * freq_pad, window), bf16),
            pltpu.SemaphoreType.DMA((4,)),
        ],
        compiler_params=pltpu.CompilerParams(vmem_limit_bytes=52 * 2**20),
        name="whiten",
    )(column[None].astype(jnp.int32), full_rows, *tables, own)

    gathered = lax.all_gather(shard, "z", axis=0, tiled=True)
    partner = lax.ppermute(gathered, "core", [(0, 1), (1, 0)])
    place = jnp.stack([z, ylo, core]).astype(jnp.int32)
    mine, theirs, scale = pl.pallas_call(
        match_kernel,
        out_shape=[jax.ShapeDtypeStruct((rows, cols), f32)] * 3,
        in_specs=[smem, vmem, vmem],
        out_specs=[vmem] * 3,
        scratch_shapes=match_scratch(),
        compiler_params=pltpu.CompilerParams(vmem_limit_bytes=32 * 2**20),
        name="match",
    )(place, gathered, partner)
    both = lax.all_gather(theirs, "ylo")
    received = lax.dynamic_index_in_dim(both, 1 - ylo, 0, keepdims=False)
    return (jnp.maximum(mine, received) * scale)[None]


def solution(mesh):
    inner = Mesh(mesh.devices.reshape(2, 16, 2, 4, 2), ("ylo", "z", "core", "x", "yhi"))
    orient, bricks = ("ylo", "z"), ("x", "yhi")
    return jax.shard_map(
        shards,
        mesh=inner,
        in_specs=(P(orient, "core", bricks), P(), P(orient, None)),
        out_specs=P(orient, "core", bricks),
        check_vma=False,
    )
```

```python
import functools
import math

import jax
import jax.numpy as jnp
import ml_dtypes
import numpy as np
from jax import lax
from jax.experimental import pallas as pl
from jax.experimental.pallas import tpu as pltpu
from jax.sharding import Mesh
from jax.sharding import PartitionSpec as P

epsilon = 1e-06
floor_share = 0.1
edge = 24
half = 12
voxels = edge**3
length = 832
cols = 104
window = 128
rows = 32
planes = 32
freqs = length // 2 + 1
freq_pad = 432
group = "ylo", "x", "yhi"
half_rows = 56
shard_rows = 2 * rows + half_rows
span = planes // 2 + edge
rots = 16
blocks = 16
depth = 32 * edge
f32 = jnp.float32
bf16 = jnp.bfloat16
f8 = jnp.float8_e4m3fn
volume_full, volume_low = 2.0**2, 2.0**11
template_full, template_low = 2.0**8, 2.0**17
nt = (((1,), (1,)), ((), ()))
tn = (((0,), (0,)), ((), ()))


def split_table(table):
    high = table.astype(ml_dtypes.bfloat16)
    low = (table - high.astype(np.float64)).astype(ml_dtypes.bfloat16)
    return high, low


@functools.cache
def dft_tables():
    freq = np.arange(freqs)
    angles = 2.0 * np.pi * ((freq[:, None] * np.arange(length)[None, :]) % length) / length
    forward = np.zeros((2, freq_pad, length))
    forward[0, :freqs] = np.cos(angles)
    forward[1, :freqs] = np.sin(angles)
    counts = np.where((freq == 0) | (freq == freqs - 1), 1.0, 2.0)[:, None] / math.sqrt(length)
    padded = np.zeros((2, freq_pad, length + edge))
    padded[0, :freqs, half : half + length] = np.cos(angles) * counts
    padded[1, :freqs, half : half + length] = np.sin(angles) * counts
    forward = forward.reshape(2 * freq_pad, length)
    padded = padded.reshape(2 * freq_pad, length + edge)
    bricks = length // cols
    backward = np.stack([padded[:, cols * j : cols * j + window] for j in range(bricks)])
    return np.stack(split_table(forward)), np.stack(split_table(backward))


def split(values):
    high = values.astype(bf16)
    low = (values - high.astype(f32)).astype(bf16)
    return high, low


def cells_of(a, b):
    if a < 20:
        return [(half * (a // 5) + b, edge * (a % 5), 0, edge)]
    if b < 8:
        return [(48 + b, edge * (a - 20), 0, edge)]
    if a < 22:
        return [(48 + 4 * (a - 20) + b - 8, 96, 0, edge)]
    return [(half * j + b - 4 * (a - 22), 120, 8 * j, 8) for j in range(3)]


def rotate_kernel(core_ref, template_ref, map_ref, out_ref, normed_ref, index_ref):
    values = template_ref[...]
    centred = values - jnp.sum(values) / voxels
    normed = centred / jnp.sqrt(jnp.sum(centred * centred) + epsilon)
    normed_ref[...] = jnp.zeros_like(normed_ref)
    for a in range(edge):
        at = slice(edge * (a // 5), edge * (a // 5 + 1))
        normed_ref[at, edge * (a % 5) : edge * (a % 5 + 1)] = normed[a]
    index_ref[...] = jnp.full_like(index_ref, -1)

    for core in range(2):

        @pl.when(core_ref[0] == core)
        def place():
            for a in range(edge):
                for b in range(half):
                    start = (a * edge + half * core + b) * edge
                    for at, lane, first, width in cells_of(a, b):
                        index_ref[at : at + 1, lane : lane + width] = map_ref[
                            0:1, start + first : start + first + width
                        ]

    def gather(i, carry):
        at = pl.ds(pl.multiple_of(8 * i, 8), 8)
        index = index_ref[at, :]
        source = jnp.maximum(index, 0)
        a = source // (edge * edge)
        rest = source - a * (edge * edge)
        b = rest // edge
        c = rest - b * edge
        group = a // 5
        lane = (a - 5 * group) * edge + c
        high = jnp.where(index < 0, -1, group * edge + b)
        totals = [jnp.zeros((8, 128), f32) for _ in range(4)]
        for row in range(5 * edge):
            table = jnp.broadcast_to(normed_ref[row : row + 1, :], (8, 128))
            found = jnp.take_along_axis(table, lane, axis=1, mode="promise_in_bounds")
            totals[row % 4] = jnp.where(high == row, found, totals[row % 4])
        out_ref[at, :] = (totals[0] + totals[1]) + (totals[2] + totals[3])
        return carry

    lax.fori_loop(0, half_rows // 8, gather, 0, unroll=7)


def whiten_kernel(
    place_ref, rows_ref, f_hbm, b_hbm, own_ref, out_ref, x_ref, fh_ref, fl_ref, bh_ref, bl_ref, sems
):
    column = place_ref[0]
    copies = [
        pltpu.make_async_copy(f_hbm.at[0], fh_ref, sems.at[0]),
        pltpu.make_async_copy(f_hbm.at[1], fl_ref, sems.at[1]),
        pltpu.make_async_copy(b_hbm.at[0, column], bh_ref, sems.at[2]),
        pltpu.make_async_copy(b_hbm.at[1, column], bl_ref, sems.at[3]),
    ]
    for copy in copies:
        copy.start()
    out_ref[0, 2 * rows :, :] = own_ref[...]
    for plane in range(2):
        for j in range(length // cols):
            x_ref[rows * plane : rows * (plane + 1), cols * j : cols * (j + 1)] = rows_ref[
                plane * 8 + j
            ]
    xh, xl = split(x_ref[...])
    copies[0].wait()
    spec = lax.dot_general(fh_ref[...], xh, nt, preferred_element_type=f32) + lax.dot_general(
        fh_ref[...], xl, nt, preferred_element_type=f32
    )
    copies[1].wait()
    spec = spec + lax.dot_general(fl_ref[...], xh, nt, preferred_element_type=f32)
    real = spec[:freq_pad]
    imag = spec[freq_pad:]
    power = real * real + imag * imag
    k = lax.broadcasted_iota(jnp.int32, power.shape, 0)
    before = jnp.where(k == 0, power[1:2], pltpu.roll(power, 1, 0))
    after = jnp.where(k == freqs - 1, power[freqs - 2 : freqs - 1], pltpu.roll(power, freq_pad - 1, 0))
    total = 2.0 * jnp.sum(power, axis=0, keepdims=True) - power[0:1] - power[freqs - 1 : freqs]
    smoothed = (before + power + after) / 3.0 + floor_share * (total / length) + epsilon
    weights = lax.rsqrt(smoothed)
    wh, wl = split(jnp.concatenate([real * weights, imag * weights], axis=0))
    copies[2].wait()
    copies[3].wait()
    out_ref[0, : 2 * rows, :] = (
        lax.dot_general(wh, bh_ref[...], tn, preferred_element_type=f32)
        + lax.dot_general(wl, bh_ref[...], tn, preferred_element_type=f32)
        + lax.dot_general(wh, bl_ref[...], tn, preferred_element_type=f32)
    )


def match_kernel(
    where_ref, own_ref, other_ref, mine_ref, theirs_ref, scale_ref, v_ref, t_ref, l_ref, l8_ref, w_ref, w8_ref, acc_ref, acc8_ref, best_ref, score_ref, next_ref
):
    z0 = where_ref[0]
    ylo = where_ref[1]
    core = where_ref[2]
    first = (core == 0).astype(f32)

    def load_plane(j, energy):
        plane = z0 - half + j
        valid = jnp.logical_and(plane >= 0, plane < planes).astype(f32)
        plane = jnp.clip(plane, 0, planes - 1)
        z = plane % 16
        start = pl.multiple_of((plane // 16) * rows, rows)
        near = other_ref[z, pl.ds(start, rows), :]
        v_ref[j, half : half + rows, :] = own_ref[z, pl.ds(start, rows), :] * valid
        v_ref[j, 0:half, :] = near[rows - half :] * (valid * (1.0 - first))
        v_ref[j, half + rows : 56, :] = near[:half] * (valid * first)
        full = v_ref[j]
        v_ref[j] = pltpu.roll(full, (j % 4) * 32, 1)
        inside = jnp.logical_and(j >= 16 * ylo, j < 16 * ylo + edge).astype(f32)
        return energy + full * full * inside

    energy = lax.fori_loop(0, span, load_plane, jnp.zeros((56, window), f32), unroll=8)

    lane = lax.broadcasted_iota(jnp.int32, (blocks, window), 1)
    place = lax.broadcasted_iota(jnp.int32, (blocks, window), 0)
    owner = ((lane + 8 * place + 8) & (window - 1)) // 32
    cell = lax.broadcasted_iota(jnp.int32, (half, window), 1)

    t_ref[...] = jnp.zeros_like(t_ref)

    def widen(sources):
        def placed(total, source, lane_from, lane_to, width):
            moved = pltpu.roll(source, (lane_to - lane_from) % window, 1)
            at = cell[: source.shape[0]]
            return jnp.where(jnp.logical_and(at >= lane_to, at < lane_to + width), moved, total)

        def step(r, carry):
            for k, source_ref in enumerate(sources):
                put = 1 + half * k
                for quad in range(6):
                    for low, high in ((0, 8), (8, half)) if quad == 5 else ((0, half),):
                        total = jnp.zeros((high - low, window), f32)
                        for part in range(4):
                            for at, lane_from, c, width in cells_of(4 * quad + part, low):
                                at = 2 * rows + at
                                source = source_ref[r, at : at + high - low, :]
                                total = placed(total, source, lane_from, 32 * part + c, width)
                        t_ref[r, quad, put + low : put + high, :] = total
            return carry

        lax.fori_loop(0, rots, step, 0, unroll=4)

    @pl.when(core == 0)
    def from_first():
        widen((own_ref, other_ref))

    @pl.when(core != 0)
    def from_second():
        widen((other_ref, own_ref))

    next_ref[...] = jnp.zeros_like(next_ref)

    def expand(step, carry):
        i = 13 - step
        here = pl.ds(pl.multiple_of(2 * blocks * i, 2 * blocks), 2 * blocks)
        for parity in range(2):
            for quad in range(span // 4):
                totals = []
                for u in range(2):
                    total = None
                    for part in range(4):
                        at = pl.ds(4 * i + 2 * u + parity, 1)
                        row = jnp.broadcast_to(v_ref[4 * quad + part, at, :], (blocks, window))
                        total = row if total is None else jnp.where(owner >= part, row, total)
                    totals.append(pltpu.roll(total, 8, 1, stride=8, stride_axis=0))
                totals.append(next_ref[parity, quad])
                next_ref[parity, quad] = totals[0]
                for tap in (parity, 2 + parity):
                    values = jnp.concatenate(totals[tap // 2 : tap // 2 + 2], axis=0)
                    high = values.astype(bf16)
                    low = ((values - high.astype(f32)) * volume_low).astype(f8)
                    full = (values * volume_full).astype(f8)
                    cell16 = window * (4 * quad + tap)
                    l_ref[here, cell16 : cell16 + window] = high
                    l8_ref[here, 2 * cell16 : 2 * cell16 + window] = low
                    l8_ref[here, 2 * cell16 + window : 2 * cell16 + 2 * window] = full
        return carry

    lax.fori_loop(0, 14, expand, 0, unroll=2)

    def build(i, slot):
        for tap in range(-1, 4):
            targets = [(tap, 0)] * (tap >= 0) + [(tap + 1, 1)] * (tap < 3)
            for four in range(rots // 4):
                for quad in range(6):
                    moved = []
                    for r in range(4 * four, 4 * four + 4):
                        row = t_ref[r, quad, pl.ds(4 * i + tap + 1, 1), :]
                        moved.append(pltpu.roll(jnp.broadcast_to(row, (8, window)), 0, 1, stride=1, stride_axis=0))
                    values = jnp.concatenate(moved, axis=0)
                    high = values.astype(bf16)
                    low = ((values - high.astype(f32)) * template_low).astype(f8)
                    full = (values * template_full).astype(f8)
                    for t, p in targets:
                        cell16 = window * (4 * quad + t)
                        at = slice(128 * p + 32 * four, 128 * p + 32 * (four + 1))
                        w_ref[slot, at, cell16 : cell16 + window] = high
                        w8_ref[slot, at, 2 * cell16 : 2 * cell16 + window] = full
                        w8_ref[slot, at, 2 * cell16 + window : 2 * cell16 + 2 * window] = low

    def product(i, slot):
        here = pl.ds(pl.multiple_of(2 * i * blocks, 2 * blocks), 16 * blocks)
        left = jnp.concatenate([l_ref[here, : 24 * window], l_ref[here, 16 * window :]], axis=0)
        acc_ref[...] += lax.dot_general(left, w_ref[slot], nt, preferred_element_type=f32)
        left = jnp.concatenate([l8_ref[here, : 48 * window], l8_ref[here, 32 * window :]], axis=0)
        acc8_ref[...] += lax.dot_general(left, w8_ref[slot], nt, preferred_element_type=f32)

    acc_ref[...] = jnp.zeros_like(acc_ref)
    acc8_ref[...] = jnp.zeros_like(acc8_ref)
    build(0, 0)

    def step(i, carry):
        build(2 * i + 1, 1)
        product(2 * i, 0)
        build(2 * i + 2, 0)
        product(2 * i + 1, 1)
        return carry

    lax.fori_loop(0, 3, step, 0)
    product(6, 0)

    lanes = lax.broadcasted_iota(jnp.int32, (16, window), 1)
    for p in range(2):
        at = slice(128 * p, 128 * (p + 1))
        best = acc_ref[:, at] + acc8_ref[:, at] * (1.0 / (volume_low * template_full))
        for shift in (64, 32, 16, 8):
            best = jnp.maximum(best, pltpu.roll(best, shift, 1))
        best_ref[...] = best
        for plane in range(2):
            score = jnp.zeros((16, window), f32)
            for block in range(13):
                found = best_ref[pl.ds(256 * plane + blocks - 1 - block, 16, stride=blocks), :]
                score = jnp.where(lanes // 8 == block, found, score)
            score_ref[pl.ds(rows * plane + p, 16, stride=2), :] = score
    mine_ref[...] = score_ref[pl.ds(pl.multiple_of(rows * ylo, rows), rows), :][:, :cols]
    theirs_ref[...] = score_ref[pl.ds(pl.multiple_of(rows * (1 - ylo), rows), rows), :][:, :cols]

    def shifted(values, count):
        return pltpu.roll(values, values.shape[0] - count, 0)

    sums = energy
    for count in (1, 2, 4):
        sums = sums + shifted(sums, count)
    sums = sums + shifted(sums, 8) + shifted(sums, 16)
    sums = sums[:rows]
    for count in (1, 2, 4):
        sums = sums + pltpu.roll(sums, window - count, 1)
    sums = sums + pltpu.roll(sums, window - 8, 1) + pltpu.roll(sums, window - 16, 1)
    scale_ref[...] = lax.rsqrt(sums / voxels + epsilon)[:, :cols]


def match_scratch():
    return [
        pltpu.VMEM((span, 56, window), f32),
        pltpu.VMEM((rots, 6, 32, window), f32),
        pltpu.VMEM((28 * blocks, 40 * window), bf16),
        pltpu.VMEM((28 * blocks, 80 * window), f8),
        pltpu.VMEM((2, 256, 24 * window), bf16),
        pltpu.VMEM((2, 256, 48 * window), f8),
        pltpu.VMEM((32 * blocks, 256), f32),
        pltpu.VMEM((32 * blocks, 256), f32),
        pltpu.VMEM((32 * blocks, 128), f32),
        pltpu.VMEM((2 * rows, 128), f32),
        pltpu.VMEM((2, span // 4, blocks, window), f32),
    ]


def shards(volume, template, voxel_maps):
    ylo, z, core = lax.axis_index("ylo"), lax.axis_index("z"), lax.axis_index("core")
    column = lax.axis_index("x") * 2 + lax.axis_index("yhi")
    vmem = pl.BlockSpec(memory_space=pltpu.VMEM)
    hbm = pl.BlockSpec(memory_space=pltpu.HBM)
    smem = pl.BlockSpec(memory_space=pltpu.SMEM)

    copies = jnp.broadcast_to(volume, (16, rows, cols))
    full_rows = lax.all_to_all(copies, group, split_axis=0, concat_axis=0, tiled=True)

    own = pl.pallas_call(
        rotate_kernel,
        out_shape=jax.ShapeDtypeStruct((half_rows, 128), f32),
        in_specs=[smem, vmem, vmem],
        out_specs=vmem,
        scratch_shapes=[pltpu.VMEM((5 * edge, 128), f32), pltpu.VMEM((half_rows, 128), jnp.int32)],
        compiler_params=pltpu.CompilerParams(vmem_limit_bytes=8 * 2**20),
        name="rotate",
    )(core[None].astype(jnp.int32), template, voxel_maps)

    tables = [jnp.asarray(table) for table in dft_tables()]
    shard = pl.pallas_call(
        whiten_kernel,
        out_shape=jax.ShapeDtypeStruct((1, shard_rows, 128), f32),
        in_specs=[smem, vmem, hbm, hbm, vmem],
        out_specs=vmem,
        scratch_shapes=[
            pltpu.VMEM((2 * rows, length), f32),
            pltpu.VMEM((2 * freq_pad, length), bf16),
            pltpu.VMEM((2 * freq_pad, length), bf16),
            pltpu.VMEM((2 * freq_pad, window), bf16),
            pltpu.VMEM((2 * freq_pad, window), bf16),
            pltpu.SemaphoreType.DMA((4,)),
        ],
        compiler_params=pltpu.CompilerParams(vmem_limit_bytes=52 * 2**20),
        name="whiten",
    )(column[None].astype(jnp.int32), full_rows, *tables, own)

    gathered = lax.all_gather(shard, "z", axis=0, tiled=True)
    partner = lax.ppermute(gathered, "core", [(0, 1), (1, 0)])
    place = jnp.stack([z, ylo, core]).astype(jnp.int32)
    mine, theirs, scale = pl.pallas_call(
        match_kernel,
        out_shape=[jax.ShapeDtypeStruct((rows, cols), f32)] * 3,
        in_specs=[smem, vmem, vmem],
        out_specs=[vmem] * 3,
        scratch_shapes=match_scratch(),
        compiler_params=pltpu.CompilerParams(vmem_limit_bytes=32 * 2**20),
        name="match",
    )(place, gathered, partner)
    both = lax.all_gather(theirs, "ylo")
    received = lax.dynamic_index_in_dim(both, 1 - ylo, 0, keepdims=False)
    return (jnp.maximum(mine, received) * scale)[None]


def solution(mesh):
    inner = Mesh(mesh.devices.reshape(2, 16, 2, 4, 2), ("ylo", "z", "core", "x", "yhi"))
    orient, bricks = ("ylo", "z"), ("x", "yhi")
    return jax.shard_map(
        shards,
        mesh=inner,
        in_specs=(P(orient, "core", bricks), P(), P(orient, None)),
        out_specs=P(orient, "core", bricks),
        check_vma=False,
    )
```

```python
import functools
import math

import jax
import jax.numpy as jnp
import ml_dtypes
import numpy as np
from jax import lax
from jax.experimental import pallas as pl
from jax.experimental.pallas import tpu as pltpu
from jax.sharding import Mesh
from jax.sharding import PartitionSpec as P

epsilon = 1e-06
floor_share = 0.1
edge = 24
half = 12
voxels = edge**3
length = 832
cols = 104
window = 128
rows = 32
planes = 32
freqs = length // 2 + 1
freq_pad = 432
group = "ylo", "x", "yhi"
half_rows = 56
shard_rows = 2 * rows + half_rows
span = planes // 2 + edge
rots = 16
blocks = 16
depth = 32 * edge
f32 = jnp.float32
bf16 = jnp.bfloat16
f8 = jnp.float8_e4m3fn
volume_full, volume_low = 2.0**2, 2.0**11
template_full, template_low = 2.0**8, 2.0**17
nt = (((1,), (1,)), ((), ()))
tn = (((0,), (0,)), ((), ()))


def split_table(table):
    high = table.astype(ml_dtypes.bfloat16)
    low = (table - high.astype(np.float64)).astype(ml_dtypes.bfloat16)
    return high, low


@functools.cache
def dft_tables():
    freq = np.arange(freqs)
    angles = 2.0 * np.pi * ((freq[:, None] * np.arange(length)[None, :]) % length) / length
    forward = np.zeros((2, freq_pad, length))
    forward[0, :freqs] = np.cos(angles)
    forward[1, :freqs] = np.sin(angles)
    counts = np.where((freq == 0) | (freq == freqs - 1), 1.0, 2.0)[:, None] / math.sqrt(length)
    padded = np.zeros((2, freq_pad, length + edge))
    padded[0, :freqs, half : half + length] = np.cos(angles) * counts
    padded[1, :freqs, half : half + length] = np.sin(angles) * counts
    forward = forward.reshape(2 * freq_pad, length)
    padded = padded.reshape(2 * freq_pad, length + edge)
    bricks = length // cols
    backward = np.stack([padded[:, cols * j : cols * j + window] for j in range(bricks)])
    return np.stack(split_table(forward)), np.stack(split_table(backward))


def split(values):
    high = values.astype(bf16)
    low = (values - high.astype(f32)).astype(bf16)
    return high, low


def cells_of(a, b):
    if a < 20:
        return [(half * (a // 5) + b, edge * (a % 5), 0, edge)]
    if b < 8:
        return [(48 + b, edge * (a - 20), 0, edge)]
    if a < 22:
        return [(48 + 4 * (a - 20) + b - 8, 96, 0, edge)]
    return [(half * j + b - 4 * (a - 22), 120, 8 * j, 8) for j in range(3)]


def rotate_kernel(core_ref, template_ref, map_ref, f_hbm, out_ref, f_ref, normed_ref, index_ref, sem):
    copy = pltpu.make_async_copy(f_hbm, f_ref, sem)
    copy.start()
    values = template_ref[...]
    centred = values - jnp.sum(values) / voxels
    normed = centred / jnp.sqrt(jnp.sum(centred * centred) + epsilon)
    normed_ref[...] = jnp.zeros_like(normed_ref)
    for a in range(edge):
        at = slice(edge * (a // 5), edge * (a // 5 + 1))
        normed_ref[at, edge * (a % 5) : edge * (a % 5 + 1)] = normed[a]
    index_ref[...] = jnp.full_like(index_ref, -1)

    for core in range(2):

        @pl.when(core_ref[0] == core)
        def place():
            for a in range(edge):
                for b in range(half):
                    start = (a * edge + half * core + b) * edge
                    for at, lane, first, width in cells_of(a, b):
                        index_ref[at : at + 1, lane : lane + width] = map_ref[
                            0:1, start + first : start + first + width
                        ]

    def gather(i, carry):
        at = pl.ds(pl.multiple_of(8 * i, 8), 8)
        index = index_ref[at, :]
        source = jnp.maximum(index, 0)
        a = source // (edge * edge)
        rest = source - a * (edge * edge)
        b = rest // edge
        c = rest - b * edge
        group = a // 5
        lane = (a - 5 * group) * edge + c
        high = jnp.where(index < 0, -1, group * edge + b)
        totals = [jnp.zeros((8, 128), f32) for _ in range(4)]
        for row in range(5 * edge):
            table = jnp.broadcast_to(normed_ref[row : row + 1, :], (8, 128))
            found = jnp.take_along_axis(table, lane, axis=1, mode="promise_in_bounds")
            totals[row % 4] = jnp.where(high == row, found, totals[row % 4])
        out_ref[at, :] = (totals[0] + totals[1]) + (totals[2] + totals[3])
        return carry

    lax.fori_loop(0, half_rows // 8, gather, 0, unroll=7)
    copy.wait()


def whiten_kernel(place_ref, rows_ref, f_ref, b_hbm, own_ref, out_ref, x_ref, bh_ref, bl_ref, sems):
    column = place_ref[0]
    copies = [
        pltpu.make_async_copy(b_hbm.at[0, column], bh_ref, sems.at[0]),
        pltpu.make_async_copy(b_hbm.at[1, column], bl_ref, sems.at[1]),
    ]
    for copy in copies:
        copy.start()
    out_ref[0, 2 * rows :, :] = own_ref[...]
    for plane in range(2):
        for j in range(length // cols):
            x_ref[rows * plane : rows * (plane + 1), cols * j : cols * (j + 1)] = rows_ref[
                plane * 8 + j
            ]
    xh, xl = split(x_ref[...])
    spec = (
        lax.dot_general(f_ref[0], xh, nt, preferred_element_type=f32)
        + lax.dot_general(f_ref[0], xl, nt, preferred_element_type=f32)
        + lax.dot_general(f_ref[1], xh, nt, preferred_element_type=f32)
    )
    real = spec[:freq_pad]
    imag = spec[freq_pad:]
    power = real * real + imag * imag
    k = lax.broadcasted_iota(jnp.int32, power.shape, 0)
    before = jnp.where(k == 0, power[1:2], pltpu.roll(power, 1, 0))
    after = jnp.where(k == freqs - 1, power[freqs - 2 : freqs - 1], pltpu.roll(power, freq_pad - 1, 0))
    total = 2.0 * jnp.sum(power, axis=0, keepdims=True) - power[0:1] - power[freqs - 1 : freqs]
    smoothed = (before + power + after) / 3.0 + floor_share * (total / length) + epsilon
    weights = lax.rsqrt(smoothed)
    wh, wl = split(jnp.concatenate([real * weights, imag * weights], axis=0))
    copies[0].wait()
    copies[1].wait()
    out_ref[0, : 2 * rows, :] = (
        lax.dot_general(wh, bh_ref[...], tn, preferred_element_type=f32)
        + lax.dot_general(wl, bh_ref[...], tn, preferred_element_type=f32)
        + lax.dot_general(wh, bl_ref[...], tn, preferred_element_type=f32)
    )


def match_kernel(
    where_ref, own_ref, other_ref, mine_ref, theirs_ref, scale_ref, v_ref, t_ref, l_ref, l8_ref, w_ref, w8_ref, acc_ref, acc8_ref, best_ref, score_ref, next_ref
):
    z0 = where_ref[0]
    ylo = where_ref[1]
    core = where_ref[2]
    first = (core == 0).astype(f32)

    def load_plane(j, energy):
        plane = z0 - half + j
        valid = jnp.logical_and(plane >= 0, plane < planes).astype(f32)
        plane = jnp.clip(plane, 0, planes - 1)
        z = plane % 16
        start = pl.multiple_of((plane // 16) * rows, rows)
        near = other_ref[z, pl.ds(start, rows), :]
        v_ref[j, half : half + rows, :] = own_ref[z, pl.ds(start, rows), :] * valid
        v_ref[j, 0:half, :] = near[rows - half :] * (valid * (1.0 - first))
        v_ref[j, half + rows : 56, :] = near[:half] * (valid * first)
        v_ref[j, 56:, :] = jnp.zeros((8, window), f32)
        full = v_ref[j, :56, :]
        v_ref[j, :56, :] = pltpu.roll(full, (j % 4) * 32, 1)
        inside = jnp.logical_and(j >= 16 * ylo, j < 16 * ylo + edge).astype(f32)
        return energy + full * full * inside

    energy = lax.fori_loop(0, span, load_plane, jnp.zeros((56, window), f32), unroll=8)

    lane = lax.broadcasted_iota(jnp.int32, (blocks, window), 1)
    place = lax.broadcasted_iota(jnp.int32, (blocks, window), 0)
    owner = ((lane + 8 * place + 8) & (window - 1)) // 32
    cell = lax.broadcasted_iota(jnp.int32, (half, window), 1)

    t_ref[...] = jnp.zeros_like(t_ref)

    def placed(total, source, lane_from, lane_to, width):
        moved = pltpu.roll(source, (lane_to - lane_from) % window, 1)
        at = cell[: source.shape[0]]
        return jnp.where(jnp.logical_and(at >= lane_to, at < lane_to + width), moved, total)

    def widen(k, r):
        mine = core == k
        put = 1 + half * k
        for quad in range(6):
            for low, high in ((0, 8), (8, half)) if quad == 5 else ((0, half),):
                total = jnp.zeros((high - low, window), f32)
                for part in range(4):
                    for at, lane_from, c, width in cells_of(4 * quad + part, low):
                        at = slice(2 * rows + at, 2 * rows + at + high - low)
                        source = jnp.where(mine, own_ref[r, at, :], other_ref[r, at, :])
                        total = placed(total, source, lane_from, 32 * part + c, width)
                t_ref[r, quad, put + low : put + high, :] = total

    def widen_first(r, carry):
        widen(0, r)
        return carry

    lax.fori_loop(0, rots, widen_first, 0, unroll=4)

    def total_of(u, parity, quad):
        total = None
        for part in range(4):
            row = jnp.broadcast_to(v_ref[4 * quad + part, pl.ds(2 * u + parity, 1), :], (blocks, window))
            total = row if total is None else jnp.where(owner >= part, row, total)
        return pltpu.roll(total, 8, 1, stride=8, stride_axis=0)

    def expand(i):
        start = 2 * blocks * i
        here = pl.ds(start if isinstance(i, int) else pl.multiple_of(start, 2 * blocks), 2 * blocks)
        for parity in range(2):
            for quad in range(span // 4):
                totals = [next_ref[parity, quad], total_of(2 * i + 1, parity, quad), total_of(2 * i + 2, parity, quad)]
                next_ref[parity, quad] = totals[2]
                for tap in (parity, 2 + parity):
                    values = jnp.concatenate(totals[tap // 2 : tap // 2 + 2], axis=0)
                    high = values.astype(bf16)
                    low = ((values - high.astype(f32)) * volume_low).astype(f8)
                    full = (values * volume_full).astype(f8)
                    cell16 = window * (4 * quad + tap)
                    l_ref[here, cell16 : cell16 + window] = high
                    l8_ref[here, 2 * cell16 : 2 * cell16 + window] = low
                    l8_ref[here, 2 * cell16 + window : 2 * cell16 + 2 * window] = full

    for parity in range(2):
        for quad in range(span // 4):
            next_ref[parity, quad] = total_of(0, parity, quad)

    def expand_first(i, carry):
        expand(i)
        return carry

    lax.fori_loop(0, 8, expand_first, 0, unroll=2)

    def build(i, slot):
        for tap in range(-1, 4):
            targets = [(tap, 0)] * (tap >= 0) + [(tap + 1, 1)] * (tap < 3)
            for four in range(rots // 4):
                for quad in range(6):
                    moved = []
                    for r in range(4 * four, 4 * four + 4):
                        row = t_ref[r, quad, 4 * i + tap + 1 : 4 * i + tap + 2, :]
                        moved.append(pltpu.roll(jnp.broadcast_to(row, (8, window)), 0, 1, stride=1, stride_axis=0))
                    values = jnp.concatenate(moved, axis=0)
                    high = values.astype(bf16)
                    low = ((values - high.astype(f32)) * template_low).astype(f8)
                    full = (values * template_full).astype(f8)
                    for t, p in targets:
                        cell16 = window * (4 * quad + t)
                        at = slice(128 * p + 32 * four, 128 * p + 32 * (four + 1))
                        w_ref[slot, at, cell16 : cell16 + window] = high
                        w8_ref[slot, at, 2 * cell16 : 2 * cell16 + window] = full
                        w8_ref[slot, at, 2 * cell16 + window : 2 * cell16 + 2 * window] = low

    def product(i, slot):
        here = slice(2 * i * blocks, (2 * i + 16) * blocks)
        left = jnp.concatenate([l_ref[here, : 24 * window], l_ref[here, 16 * window :]], axis=0)
        acc_ref[...] += lax.dot_general(left, w_ref[slot], nt, preferred_element_type=f32)
        left = jnp.concatenate([l8_ref[here, : 48 * window], l8_ref[here, 32 * window :]], axis=0)
        acc8_ref[...] += lax.dot_general(left, w8_ref[slot], nt, preferred_element_type=f32)

    acc_ref[...] = jnp.zeros_like(acc_ref)
    acc8_ref[...] = jnp.zeros_like(acc8_ref)
    build(0, 0)
    for i in range(7):
        if i < 2:
            for r in range(8 * i, 8 * i + 8):
                widen(1, r)
        if i < 6:
            build(i + 1, (i + 1) % 2)
            expand(8 + i)
        product(i, i % 2)

    lanes = lax.broadcasted_iota(jnp.int32, (16, window), 1)
    for p in range(2):
        at = slice(128 * p, 128 * (p + 1))
        best = acc_ref[:, at] + acc8_ref[:, at] * (1.0 / (volume_low * template_full))
        for shift in (64, 32, 16, 8):
            best = jnp.maximum(best, pltpu.roll(best, shift, 1))
        best_ref[...] = best
        for plane in range(2):
            score = jnp.zeros((16, window), f32)
            for block in range(13):
                found = best_ref[pl.ds(256 * plane + blocks - 1 - block, 16, stride=blocks), :]
                score = jnp.where(lanes // 8 == block, found, score)
            score_ref[pl.ds(rows * plane + p, 16, stride=2), :] = score
    mine_ref[...] = score_ref[pl.ds(pl.multiple_of(rows * ylo, rows), rows), :][:, :cols]
    theirs_ref[...] = score_ref[pl.ds(pl.multiple_of(rows * (1 - ylo), rows), rows), :][:, :cols]

    def shifted(values, count):
        return pltpu.roll(values, values.shape[0] - count, 0)

    sums = energy
    for count in (1, 2, 4):
        sums = sums + shifted(sums, count)
    sums = sums + shifted(sums, 8) + shifted(sums, 16)
    sums = sums[:rows]
    for count in (1, 2, 4):
        sums = sums + pltpu.roll(sums, window - count, 1)
    sums = sums + pltpu.roll(sums, window - 8, 1) + pltpu.roll(sums, window - 16, 1)
    scale_ref[...] = lax.rsqrt(sums / voxels + epsilon)[:, :cols]


def match_scratch():
    return [
        pltpu.VMEM((span, 64, window), f32),
        pltpu.VMEM((rots, 6, 32, window), f32),
        pltpu.VMEM((28 * blocks, 40 * window), bf16),
        pltpu.VMEM((28 * blocks, 80 * window), f8),
        pltpu.VMEM((2, 256, 24 * window), bf16),
        pltpu.VMEM((2, 256, 48 * window), f8),
        pltpu.VMEM((32 * blocks, 256), f32),
        pltpu.VMEM((32 * blocks, 256), f32),
        pltpu.VMEM((32 * blocks, 128), f32),
        pltpu.VMEM((2 * rows, 128), f32),
        pltpu.VMEM((2, span // 4, blocks, window), f32),
    ]


def shards(volume, template, voxel_maps):
    ylo, z, core = lax.axis_index("ylo"), lax.axis_index("z"), lax.axis_index("core")
    column = lax.axis_index("x") * 2 + lax.axis_index("yhi")
    vmem = pl.BlockSpec(memory_space=pltpu.VMEM)
    hbm = pl.BlockSpec(memory_space=pltpu.HBM)
    smem = pl.BlockSpec(memory_space=pltpu.SMEM)

    copies = jnp.broadcast_to(volume, (16, rows, cols))
    full_rows = lax.all_to_all(copies, group, split_axis=0, concat_axis=0, tiled=True)

    forward, backward = (jnp.asarray(table) for table in dft_tables())
    own, forward = pl.pallas_call(
        rotate_kernel,
        out_shape=[
            jax.ShapeDtypeStruct((half_rows, 128), f32),
            jax.ShapeDtypeStruct((2, 2 * freq_pad, length), bf16),
        ],
        in_specs=[smem, vmem, vmem, hbm],
        out_specs=[vmem] * 2,
        scratch_shapes=[
            pltpu.VMEM((5 * edge, 128), f32),
            pltpu.VMEM((half_rows, 128), jnp.int32),
            pltpu.SemaphoreType.DMA,
        ],
        compiler_params=pltpu.CompilerParams(vmem_limit_bytes=48 * 2**20),
        name="rotate",
    )(core[None].astype(jnp.int32), template, voxel_maps, forward)
    shard = pl.pallas_call(
        whiten_kernel,
        out_shape=jax.ShapeDtypeStruct((1, shard_rows, 128), f32),
        in_specs=[smem, vmem, vmem, hbm, vmem],
        out_specs=vmem,
        scratch_shapes=[
            pltpu.VMEM((2 * rows, length), f32),
            pltpu.VMEM((2 * freq_pad, window), bf16),
            pltpu.VMEM((2 * freq_pad, window), bf16),
            pltpu.SemaphoreType.DMA((2,)),
        ],
        compiler_params=pltpu.CompilerParams(vmem_limit_bytes=50 * 2**20),
        name="whiten",
    )(column[None].astype(jnp.int32), full_rows, forward, backward, own)

    gathered = lax.all_gather(shard, "z", axis=0, tiled=True)
    partner = lax.ppermute(gathered, "core", [(0, 1), (1, 0)])
    place = jnp.stack([z, ylo, core]).astype(jnp.int32)
    mine, theirs, scale = pl.pallas_call(
        match_kernel,
        out_shape=[jax.ShapeDtypeStruct((rows, cols), f32)] * 3,
        in_specs=[smem, vmem, vmem],
        out_specs=[vmem] * 3,
        scratch_shapes=match_scratch(),
        compiler_params=pltpu.CompilerParams(vmem_limit_bytes=32 * 2**20),
        name="match",
    )(place, gathered, partner)
    both = lax.all_gather(theirs, "ylo")
    received = lax.dynamic_index_in_dim(both, 1 - ylo, 0, keepdims=False)
    return (jnp.maximum(mine, received) * scale)[None]


def solution(mesh):
    inner = Mesh(mesh.devices.reshape(2, 16, 2, 4, 2), ("ylo", "z", "core", "x", "yhi"))
    orient, bricks = ("ylo", "z"), ("x", "yhi")
    return jax.shard_map(
        shards,
        mesh=inner,
        in_specs=(P(orient, "core", bricks), P(), P(orient, None)),
        out_specs=P(orient, "core", bricks),
        check_vma=False,
    )
```

```python
import functools
import math

import jax
import jax.numpy as jnp
import ml_dtypes
import numpy as np
from jax import lax
from jax.experimental import pallas as pl
from jax.experimental.pallas import tpu as pltpu
from jax.sharding import Mesh
from jax.sharding import PartitionSpec as P

epsilon = 1e-06
floor_share = 0.1
edge = 24
half = 12
voxels = edge**3
length = 832
cols = 104
window = 128
rows = 32
planes = 32
freqs = length // 2 + 1
freq_pad = 432
group = "ylo", "x", "yhi"
half_rows = 56
shard_rows = 2 * rows + half_rows
span = planes // 2 + edge
rots = 16
blocks = 16
depth = 32 * edge
f32 = jnp.float32
bf16 = jnp.bfloat16
f8 = jnp.float8_e4m3fn
volume_full, volume_low = 2.0**2, 2.0**11
template_full, template_low = 2.0**8, 2.0**17
nt = (((1,), (1,)), ((), ()))
tn = (((0,), (0,)), ((), ()))


def split_table(table):
    high = table.astype(ml_dtypes.bfloat16)
    low = (table - high.astype(np.float64)).astype(ml_dtypes.bfloat16)
    return high, low


@functools.cache
def dft_tables():
    freq = np.arange(freqs)
    angles = 2.0 * np.pi * ((freq[:, None] * np.arange(length)[None, :]) % length) / length
    forward = np.zeros((2, freq_pad, length))
    forward[0, :freqs] = np.cos(angles)
    forward[1, :freqs] = np.sin(angles)
    counts = np.where((freq == 0) | (freq == freqs - 1), 1.0, 2.0)[:, None] / math.sqrt(length)
    padded = np.zeros((2, freq_pad, length + edge))
    padded[0, :freqs, half : half + length] = np.cos(angles) * counts
    padded[1, :freqs, half : half + length] = np.sin(angles) * counts
    forward = forward.reshape(2 * freq_pad, length)
    padded = padded.reshape(2 * freq_pad, length + edge)
    bricks = length // cols
    backward = np.stack([padded[:, cols * j : cols * j + window] for j in range(bricks)])
    return np.stack(split_table(forward)), np.stack(split_table(backward))


def split(values):
    high = values.astype(bf16)
    low = (values - high.astype(f32)).astype(bf16)
    return high, low


def cells_of(a, b):
    if a < 20:
        return [(half * (a // 5) + b, edge * (a % 5), 0, edge)]
    if b < 8:
        return [(48 + b, edge * (a - 20), 0, edge)]
    if a < 22:
        return [(48 + 4 * (a - 20) + b - 8, 96, 0, edge)]
    return [(half * j + b - 4 * (a - 22), 120, 8 * j, 8) for j in range(3)]


def rotate_kernel(core_ref, template_ref, map_ref, f_hbm, out_ref, f_ref, normed_ref, index_ref, sem):
    copy = pltpu.make_async_copy(f_hbm, f_ref, sem)
    copy.start()
    values = template_ref[...]
    centred = values - jnp.sum(values) / voxels
    normed = centred / jnp.sqrt(jnp.sum(centred * centred) + epsilon)
    normed_ref[...] = jnp.zeros_like(normed_ref)
    for a in range(edge):
        at = slice(edge * (a // 5), edge * (a // 5 + 1))
        normed_ref[at, edge * (a % 5) : edge * (a % 5 + 1)] = normed[a]
    index_ref[...] = jnp.full_like(index_ref, -1)

    for core in range(2):

        @pl.when(core_ref[0] == core)
        def place():
            for a in range(edge):
                for b in range(half):
                    start = (a * edge + half * core + b) * edge
                    for at, lane, first, width in cells_of(a, b):
                        index_ref[at : at + 1, lane : lane + width] = map_ref[
                            0:1, start + first : start + first + width
                        ]

    def gather(i, carry):
        at = pl.ds(pl.multiple_of(8 * i, 8), 8)
        index = index_ref[at, :]
        source = jnp.maximum(index, 0)
        a = source // (edge * edge)
        rest = source - a * (edge * edge)
        b = rest // edge
        c = rest - b * edge
        group = a // 5
        lane = (a - 5 * group) * edge + c
        high = jnp.where(index < 0, -1, group * edge + b)
        totals = [jnp.zeros((8, 128), f32) for _ in range(4)]
        for row in range(5 * edge):
            table = jnp.broadcast_to(normed_ref[row : row + 1, :], (8, 128))
            found = jnp.take_along_axis(table, lane, axis=1, mode="promise_in_bounds")
            totals[row % 4] = jnp.where(high == row, found, totals[row % 4])
        out_ref[at, :] = (totals[0] + totals[1]) + (totals[2] + totals[3])
        return carry

    lax.fori_loop(0, half_rows // 8, gather, 0, unroll=7)
    copy.wait()


def whiten_kernel(place_ref, rows_ref, f_ref, b_hbm, own_ref, out_ref, x_ref, bh_ref, bl_ref, sems):
    column = place_ref[0]
    copies = [
        pltpu.make_async_copy(b_hbm.at[0, column], bh_ref, sems.at[0]),
        pltpu.make_async_copy(b_hbm.at[1, column], bl_ref, sems.at[1]),
    ]
    for copy in copies:
        copy.start()
    out_ref[0, 2 * rows :, :] = own_ref[...]
    for plane in range(2):
        for j in range(length // cols):
            x_ref[rows * plane : rows * (plane + 1), cols * j : cols * (j + 1)] = rows_ref[
                plane * 8 + j
            ]
    xh, xl = split(x_ref[...])
    spec = (
        lax.dot_general(f_ref[0], xh, nt, preferred_element_type=f32)
        + lax.dot_general(f_ref[0], xl, nt, preferred_element_type=f32)
        + lax.dot_general(f_ref[1], xh, nt, preferred_element_type=f32)
    )
    real = spec[:freq_pad]
    imag = spec[freq_pad:]
    power = real * real + imag * imag
    k = lax.broadcasted_iota(jnp.int32, power.shape, 0)
    before = jnp.where(k == 0, power[1:2], pltpu.roll(power, 1, 0))
    after = jnp.where(k == freqs - 1, power[freqs - 2 : freqs - 1], pltpu.roll(power, freq_pad - 1, 0))
    total = 2.0 * jnp.sum(power, axis=0, keepdims=True) - power[0:1] - power[freqs - 1 : freqs]
    smoothed = (before + power + after) / 3.0 + floor_share * (total / length) + epsilon
    weights = lax.rsqrt(smoothed)
    wh, wl = split(jnp.concatenate([real * weights, imag * weights], axis=0))
    copies[0].wait()
    copies[1].wait()
    out_ref[0, : 2 * rows, :] = (
        lax.dot_general(wh, bh_ref[...], tn, preferred_element_type=f32)
        + lax.dot_general(wl, bh_ref[...], tn, preferred_element_type=f32)
        + lax.dot_general(wh, bl_ref[...], tn, preferred_element_type=f32)
    )


def match_kernel(
    where_ref, own_ref, other_ref, mine_ref, theirs_ref, scale_ref, v_ref, t_ref, l_ref, l8_ref, w_ref, w8_ref, acc_ref, acc8_ref, best_ref, score_ref, next_ref
):
    z0 = where_ref[0]
    ylo = where_ref[1]
    core = where_ref[2]
    first = (core == 0).astype(f32)

    def load_plane(j, energy):
        plane = z0 - half + j
        valid = jnp.logical_and(plane >= 0, plane < planes).astype(f32)
        plane = jnp.clip(plane, 0, planes - 1)
        z = plane % 16
        start = pl.multiple_of((plane // 16) * rows, rows)
        near = other_ref[z, pl.ds(start, rows), :]
        v_ref[j, half : half + rows, :] = own_ref[z, pl.ds(start, rows), :] * valid
        v_ref[j, 0:half, :] = near[rows - half :] * (valid * (1.0 - first))
        v_ref[j, half + rows : 56, :] = near[:half] * (valid * first)
        v_ref[j, 56:, :] = jnp.zeros((8, window), f32)
        full = v_ref[j, :56, :]
        v_ref[j, :56, :] = pltpu.roll(full, (j % 4) * 32, 1)
        inside = jnp.logical_and(j >= 16 * ylo, j < 16 * ylo + edge).astype(f32)
        return energy + full * full * inside

    energy = lax.fori_loop(0, span, load_plane, jnp.zeros((56, window), f32), unroll=8)

    lane = lax.broadcasted_iota(jnp.int32, (blocks, window), 1)
    place = lax.broadcasted_iota(jnp.int32, (blocks, window), 0)
    owner = ((lane + 8 * place + 8) & (window - 1)) // 32
    cell = lax.broadcasted_iota(jnp.int32, (half, window), 1)

    t_ref[...] = jnp.zeros_like(t_ref)

    def placed(total, source, lane_from, lane_to, width):
        moved = pltpu.roll(source, (lane_to - lane_from) % window, 1)
        at = cell[: source.shape[0]]
        return jnp.where(jnp.logical_and(at >= lane_to, at < lane_to + width), moved, total)

    def widen(k, r):
        mine = core == k
        put = 1 + half * k
        for quad in range(6):
            for low, high in ((0, 8), (8, half)) if quad == 5 else ((0, half),):
                total = jnp.zeros((high - low, window), f32)
                for part in range(4):
                    for at, lane_from, c, width in cells_of(4 * quad + part, low):
                        at = slice(2 * rows + at, 2 * rows + at + high - low)
                        source = jnp.where(mine, own_ref[r, at, :], other_ref[r, at, :])
                        total = placed(total, source, lane_from, 32 * part + c, width)
                t_ref[r, quad, put + low : put + high, :] = total

    def widen_first(r, carry):
        widen(0, r)
        return carry

    lax.fori_loop(0, rots, widen_first, 0, unroll=4)

    def total_of(u, parity, quad):
        total = None
        for part in range(4):
            row = jnp.broadcast_to(v_ref[4 * quad + part, pl.ds(2 * u + parity, 1), :], (blocks, window))
            total = row if total is None else jnp.where(owner >= part, row, total)
        return pltpu.roll(total, 8, 1, stride=8, stride_axis=0)

    def expand(i):
        start = 2 * blocks * i
        here = pl.ds(start if isinstance(i, int) else pl.multiple_of(start, 2 * blocks), 2 * blocks)
        for parity in range(2):
            for quad in range(span // 4):
                totals = [next_ref[parity, quad], total_of(2 * i + 1, parity, quad), total_of(2 * i + 2, parity, quad)]
                next_ref[parity, quad] = totals[2]
                for tap in (parity, 2 + parity):
                    values = jnp.concatenate(totals[tap // 2 : tap // 2 + 2], axis=0)
                    high = values.astype(bf16)
                    low = ((values - high.astype(f32)) * volume_low).astype(f8)
                    full = (values * volume_full).astype(f8)
                    cell16 = window * (4 * quad + tap)
                    l_ref[here, cell16 : cell16 + window] = high
                    l8_ref[here, 2 * cell16 : 2 * cell16 + window] = low
                    l8_ref[here, 2 * cell16 + window : 2 * cell16 + 2 * window] = full

    for parity in range(2):
        for quad in range(span // 4):
            next_ref[parity, quad] = total_of(0, parity, quad)

    def expand_first(i, carry):
        expand(i)
        return carry

    lax.fori_loop(0, 8, expand_first, 0, unroll=2)

    def build(i, slot):
        for tap in range(-1, 4 if i < 6 else 1):
            targets = [(tap, 0)] * (tap >= 0) + [(tap + 1, 1)] * (tap < 3)
            targets = [(t, p) for t, p in targets if i < 6 or t == 0]
            for four in range(rots // 4):
                for quad in range(6):
                    moved = []
                    for r in range(4 * four, 4 * four + 4):
                        row = t_ref[r, quad, 4 * i + tap + 1 : 4 * i + tap + 2, :]
                        moved.append(pltpu.roll(jnp.broadcast_to(row, (8, window)), 0, 1, stride=1, stride_axis=0))
                    values = jnp.concatenate(moved, axis=0)
                    high = values.astype(bf16)
                    low = ((values - high.astype(f32)) * template_low).astype(f8)
                    full = (values * template_full).astype(f8)
                    for t, p in targets:
                        cell16 = window * (4 * quad + t)
                        at = slice(128 * p + 32 * four, 128 * p + 32 * (four + 1))
                        w_ref[slot, at, cell16 : cell16 + window] = high
                        w8_ref[slot, at, 2 * cell16 : 2 * cell16 + window] = full
                        w8_ref[slot, at, 2 * cell16 + window : 2 * cell16 + 2 * window] = low

    def product(steps):
        for left_ref, right_ref, sum_ref, wide in (
            (l_ref, w_ref, acc_ref, window),
            (l8_ref, w8_ref, acc8_ref, 2 * window),
        ):
            left, right = ([], []), []
            for i in steps:
                here = slice(2 * i * blocks, (2 * i + 16) * blocks)
                pieces = [(0, 24 * wide)] if i < 6 else [(4 * quad * wide, wide) for quad in range(6)]
                for start, size in pieces:
                    for plane in range(2):
                        at = start + 16 * plane * wide
                        left[plane].append(left_ref[here, at : at + size])
                    right.append(right_ref[i % 4, :, start : start + size])
            both = jnp.concatenate([jnp.concatenate(part, axis=1) for part in left], axis=0)
            sum_ref[...] += lax.dot_general(
                both, jnp.concatenate(right, axis=1), nt, preferred_element_type=f32
            )

    acc_ref[...] = jnp.zeros_like(acc_ref)
    acc8_ref[...] = jnp.zeros_like(acc8_ref)
    build(0, 0)
    groups = (0,), (1, 2), (3, 4), (5, 6)
    for k, group in enumerate(groups):
        if k == 1:
            for r in range(rots):
                widen(1, r)
        for i in groups[k + 1] if k < 3 else ():
            build(i, i % 4)
            expand(i + 7)
        product(group)

    lanes = lax.broadcasted_iota(jnp.int32, (16, window), 1)
    for p in range(2):
        at = slice(128 * p, 128 * (p + 1))
        best = acc_ref[:, at] + acc8_ref[:, at] * (1.0 / (volume_low * template_full))
        for shift in (64, 32, 16, 8):
            best = jnp.maximum(best, pltpu.roll(best, shift, 1))
        best_ref[...] = best
        for plane in range(2):
            score = jnp.zeros((16, window), f32)
            for block in range(13):
                found = best_ref[pl.ds(256 * plane + blocks - 1 - block, 16, stride=blocks), :]
                score = jnp.where(lanes // 8 == block, found, score)
            score_ref[pl.ds(rows * plane + p, 16, stride=2), :] = score
    mine_ref[...] = score_ref[pl.ds(pl.multiple_of(rows * ylo, rows), rows), :][:, :cols]
    theirs_ref[...] = score_ref[pl.ds(pl.multiple_of(rows * (1 - ylo), rows), rows), :][:, :cols]

    def shifted(values, count):
        return pltpu.roll(values, values.shape[0] - count, 0)

    sums = energy
    for count in (1, 2, 4):
        sums = sums + shifted(sums, count)
    sums = sums + shifted(sums, 8) + shifted(sums, 16)
    sums = sums[:rows]
    for count in (1, 2, 4):
        sums = sums + pltpu.roll(sums, window - count, 1)
    sums = sums + pltpu.roll(sums, window - 8, 1) + pltpu.roll(sums, window - 16, 1)
    scale_ref[...] = lax.rsqrt(sums / voxels + epsilon)[:, :cols]


def match_scratch():
    return [
        pltpu.VMEM((span, 64, window), f32),
        pltpu.VMEM((rots, 6, 32, window), f32),
        pltpu.VMEM((28 * blocks, 40 * window), bf16),
        pltpu.VMEM((28 * blocks, 80 * window), f8),
        pltpu.VMEM((4, 256, 24 * window), bf16),
        pltpu.VMEM((4, 256, 48 * window), f8),
        pltpu.VMEM((32 * blocks, 256), f32),
        pltpu.VMEM((32 * blocks, 256), f32),
        pltpu.VMEM((32 * blocks, 128), f32),
        pltpu.VMEM((2 * rows, 128), f32),
        pltpu.VMEM((2, span // 4, blocks, window), f32),
    ]


def shards(volume, template, voxel_maps):
    ylo, z, core = lax.axis_index("ylo"), lax.axis_index("z"), lax.axis_index("core")
    column = lax.axis_index("x") * 2 + lax.axis_index("yhi")
    vmem = pl.BlockSpec(memory_space=pltpu.VMEM)
    hbm = pl.BlockSpec(memory_space=pltpu.HBM)
    smem = pl.BlockSpec(memory_space=pltpu.SMEM)

    copies = jnp.broadcast_to(volume, (16, rows, cols))
    full_rows = lax.all_to_all(copies, group, split_axis=0, concat_axis=0, tiled=True)

    forward, backward = (jnp.asarray(table) for table in dft_tables())
    own, forward = pl.pallas_call(
        rotate_kernel,
        out_shape=[
            jax.ShapeDtypeStruct((half_rows, 128), f32),
            jax.ShapeDtypeStruct((2, 2 * freq_pad, length), bf16),
        ],
        in_specs=[smem, vmem, vmem, hbm],
        out_specs=[vmem] * 2,
        scratch_shapes=[
            pltpu.VMEM((5 * edge, 128), f32),
            pltpu.VMEM((half_rows, 128), jnp.int32),
            pltpu.SemaphoreType.DMA,
        ],
        compiler_params=pltpu.CompilerParams(vmem_limit_bytes=48 * 2**20),
        name="rotate",
    )(core[None].astype(jnp.int32), template, voxel_maps, forward)
    shard = pl.pallas_call(
        whiten_kernel,
        out_shape=jax.ShapeDtypeStruct((1, shard_rows, 128), f32),
        in_specs=[smem, vmem, vmem, hbm, vmem],
        out_specs=vmem,
        scratch_shapes=[
            pltpu.VMEM((2 * rows, length), f32),
            pltpu.VMEM((2 * freq_pad, window), bf16),
            pltpu.VMEM((2 * freq_pad, window), bf16),
            pltpu.SemaphoreType.DMA((2,)),
        ],
        compiler_params=pltpu.CompilerParams(vmem_limit_bytes=50 * 2**20),
        name="whiten",
    )(column[None].astype(jnp.int32), full_rows, forward, backward, own)

    gathered = lax.all_gather(shard, "z", axis=0, tiled=True)
    partner = lax.ppermute(gathered, "core", [(0, 1), (1, 0)])
    place = jnp.stack([z, ylo, core]).astype(jnp.int32)
    mine, theirs, scale = pl.pallas_call(
        match_kernel,
        out_shape=[jax.ShapeDtypeStruct((rows, cols), f32)] * 3,
        in_specs=[smem, vmem, vmem],
        out_specs=[vmem] * 3,
        scratch_shapes=match_scratch(),
        compiler_params=pltpu.CompilerParams(vmem_limit_bytes=44 * 2**20),
        name="match",
    )(place, gathered, partner)
    both = lax.all_gather(theirs, "ylo")
    received = lax.dynamic_index_in_dim(both, 1 - ylo, 0, keepdims=False)
    return (jnp.maximum(mine, received) * scale)[None]


def solution(mesh):
    inner = Mesh(mesh.devices.reshape(2, 16, 2, 4, 2), ("ylo", "z", "core", "x", "yhi"))
    orient, bricks = ("ylo", "z"), ("x", "yhi")
    return jax.shard_map(
        shards,
        mesh=inner,
        in_specs=(P(orient, "core", bricks), P(), P(orient, None)),
        out_specs=P(orient, "core", bricks),
        check_vma=False,
    )
```

```python
import functools
import math

import jax
import jax.numpy as jnp
import ml_dtypes
import numpy as np
from jax import lax
from jax.experimental import pallas as pl
from jax.experimental.pallas import tpu as pltpu
from jax.sharding import Mesh
from jax.sharding import PartitionSpec as P

epsilon = 1e-06
floor_share = 0.1
edge = 24
half = 12
voxels = edge**3
length = 832
cols = 104
window = 128
rows = 32
planes = 32
freqs = length // 2 + 1
freq_pad = 432
group = "ylo", "x", "yhi"
half_rows = 56
shard_rows = 2 * rows + half_rows
span = planes // 2 + edge
rots = 16
blocks = 16
depth = 32 * edge
f32 = jnp.float32
bf16 = jnp.bfloat16
f8 = jnp.float8_e4m3fn
volume_full, volume_low = 2.0**2, 2.0**11
template_full, template_low = 2.0**8, 2.0**17
nt = (((1,), (1,)), ((), ()))
tn = (((0,), (0,)), ((), ()))


def split_table(table):
    high = table.astype(ml_dtypes.bfloat16)
    low = (table - high.astype(np.float64)).astype(ml_dtypes.bfloat16)
    return high, low


@functools.cache
def dft_tables():
    freq = np.arange(freqs)
    angles = 2.0 * np.pi * ((freq[:, None] * np.arange(length)[None, :]) % length) / length
    forward = np.zeros((2, freq_pad, length))
    forward[0, :freqs] = np.cos(angles)
    forward[1, :freqs] = np.sin(angles)
    counts = np.where((freq == 0) | (freq == freqs - 1), 1.0, 2.0)[:, None] / math.sqrt(length)
    padded = np.zeros((2, freq_pad, length + edge))
    padded[0, :freqs, half : half + length] = np.cos(angles) * counts
    padded[1, :freqs, half : half + length] = np.sin(angles) * counts
    forward = forward.reshape(2 * freq_pad, length)
    padded = padded.reshape(2 * freq_pad, length + edge)
    bricks = length // cols
    backward = np.stack([padded[:, cols * j : cols * j + window] for j in range(bricks)])
    return np.stack(split_table(forward)), np.stack(split_table(backward))


def split(values):
    high = values.astype(bf16)
    low = (values - high.astype(f32)).astype(bf16)
    return high, low


def cells_of(a, b):
    if a < 20:
        return [(half * (a // 5) + b, edge * (a % 5), 0, edge)]
    if b < 8:
        return [(48 + b, edge * (a - 20), 0, edge)]
    if a < 22:
        return [(48 + 4 * (a - 20) + b - 8, 96, 0, edge)]
    return [(half * j + b - 4 * (a - 22), 120, 8 * j, 8) for j in range(3)]


def rotate_kernel(core_ref, template_ref, map_ref, f_hbm, out_ref, f_ref, normed_ref, index_ref, sem):
    copy = pltpu.make_async_copy(f_hbm, f_ref, sem)
    copy.start()
    values = template_ref[...]
    centred = values - jnp.sum(values) / voxels
    normed = centred / jnp.sqrt(jnp.sum(centred * centred) + epsilon)
    normed_ref[...] = jnp.zeros_like(normed_ref)
    for a in range(edge):
        at = slice(edge * (a // 5), edge * (a // 5 + 1))
        normed_ref[at, edge * (a % 5) : edge * (a % 5 + 1)] = normed[a]
    index_ref[...] = jnp.full_like(index_ref, -1)

    for core in range(2):

        @pl.when(core_ref[0] == core)
        def place():
            for a in range(edge):
                for b in range(half):
                    start = (a * edge + half * core + b) * edge
                    for at, lane, first, width in cells_of(a, b):
                        index_ref[at : at + 1, lane : lane + width] = map_ref[
                            0:1, start + first : start + first + width
                        ]

    def gather(i, carry):
        at = pl.ds(pl.multiple_of(8 * i, 8), 8)
        index = index_ref[at, :]
        source = jnp.maximum(index, 0)
        a = source // (edge * edge)
        rest = source - a * (edge * edge)
        b = rest // edge
        c = rest - b * edge
        group = a // 5
        lane = (a - 5 * group) * edge + c
        high = jnp.where(index < 0, -1, group * edge + b)
        totals = [jnp.zeros((8, 128), f32) for _ in range(4)]
        for row in range(5 * edge):
            table = jnp.broadcast_to(normed_ref[row : row + 1, :], (8, 128))
            found = jnp.take_along_axis(table, lane, axis=1, mode="promise_in_bounds")
            totals[row % 4] = jnp.where(high == row, found, totals[row % 4])
        out_ref[at, :] = (totals[0] + totals[1]) + (totals[2] + totals[3])
        return carry

    lax.fori_loop(0, half_rows // 8, gather, 0, unroll=7)
    copy.wait()


def whiten_kernel(place_ref, rows_ref, f_ref, b_hbm, own_ref, out_ref, x_ref, bh_ref, bl_ref, sems):
    column = place_ref[0]
    copies = [
        pltpu.make_async_copy(b_hbm.at[0, column], bh_ref, sems.at[0]),
        pltpu.make_async_copy(b_hbm.at[1, column], bl_ref, sems.at[1]),
    ]
    for copy in copies:
        copy.start()
    out_ref[0, 2 * rows :, :] = own_ref[...]
    for plane in range(2):
        for j in range(length // cols):
            x_ref[rows * plane : rows * (plane + 1), cols * j : cols * (j + 1)] = rows_ref[
                plane * 8 + j
            ]
    xh, xl = split(x_ref[...])
    spec = (
        lax.dot_general(f_ref[0], xh, nt, preferred_element_type=f32)
        + lax.dot_general(f_ref[0], xl, nt, preferred_element_type=f32)
        + lax.dot_general(f_ref[1], xh, nt, preferred_element_type=f32)
    )
    real = spec[:freq_pad]
    imag = spec[freq_pad:]
    power = real * real + imag * imag
    k = lax.broadcasted_iota(jnp.int32, power.shape, 0)
    before = jnp.where(k == 0, power[1:2], pltpu.roll(power, 1, 0))
    after = jnp.where(k == freqs - 1, power[freqs - 2 : freqs - 1], pltpu.roll(power, freq_pad - 1, 0))
    total = 2.0 * jnp.sum(power, axis=0, keepdims=True) - power[0:1] - power[freqs - 1 : freqs]
    smoothed = (before + power + after) / 3.0 + floor_share * (total / length) + epsilon
    weights = lax.rsqrt(smoothed)
    wh, wl = split(jnp.concatenate([real * weights, imag * weights], axis=0))
    copies[0].wait()
    copies[1].wait()
    out_ref[0, : 2 * rows, :] = (
        lax.dot_general(wh, bh_ref[...], tn, preferred_element_type=f32)
        + lax.dot_general(wl, bh_ref[...], tn, preferred_element_type=f32)
        + lax.dot_general(wh, bl_ref[...], tn, preferred_element_type=f32)
    )


def match_kernel(
    where_ref, own_ref, other_ref, mine_ref, theirs_ref, scale_ref, v_ref, t_ref, l_ref, l8_ref, w_ref, w8_ref, acc_ref, acc8_ref, best_ref, score_ref, next_ref
):
    z0 = where_ref[0]
    ylo = where_ref[1]
    core = where_ref[2]
    first = (core == 0).astype(f32)

    def load_plane(j, energy):
        plane = z0 - half + j
        valid = jnp.logical_and(plane >= 0, plane < planes).astype(f32)
        plane = jnp.clip(plane, 0, planes - 1)
        z = plane % 16
        start = pl.multiple_of((plane // 16) * rows, rows)
        near = other_ref[z, pl.ds(start, rows), :]
        v_ref[j, half : half + rows, :] = own_ref[z, pl.ds(start, rows), :] * valid
        v_ref[j, 0:half, :] = near[rows - half :] * (valid * (1.0 - first))
        v_ref[j, half + rows : 56, :] = near[:half] * (valid * first)
        v_ref[j, 56:, :] = jnp.zeros((8, window), f32)
        full = v_ref[j, :56, :]
        v_ref[j, :56, :] = pltpu.roll(full, (j % 4) * 32, 1)
        inside = jnp.logical_and(j >= 16 * ylo, j < 16 * ylo + edge).astype(f32)
        return energy + full * full * inside

    energy = lax.fori_loop(0, span, load_plane, jnp.zeros((56, window), f32), unroll=8)

    lane = lax.broadcasted_iota(jnp.int32, (blocks, window), 1)
    place = lax.broadcasted_iota(jnp.int32, (blocks, window), 0)
    owner = ((lane + 8 * place + 8) & (window - 1)) // 32
    cell = lax.broadcasted_iota(jnp.int32, (half, window), 1)

    t_ref[:, :, :8, :] = jnp.zeros((rots, 6, 8, window), f32)
    t_ref[:, :, 24:, :] = jnp.zeros((rots, 6, 8, window), f32)

    def placed(total, source, lane_from, lane_to, width):
        moved = pltpu.roll(source, (lane_to - lane_from) % window, 1)
        at = cell[: source.shape[0]]
        return jnp.where(jnp.logical_and(at >= lane_to, at < lane_to + width), moved, total)

    def widen(k, r):
        mine = core == k
        put = 1 + half * k
        for quad in range(6):
            for low, high in ((0, 8), (8, half)) if quad == 5 else ((0, half),):
                total = jnp.zeros((high - low, window), f32)
                for part in range(4):
                    for at, lane_from, c, width in cells_of(4 * quad + part, low):
                        at = slice(2 * rows + at, 2 * rows + at + high - low)
                        source = jnp.where(mine, own_ref[r, at, :], other_ref[r, at, :])
                        total = placed(total, source, lane_from, 32 * part + c, width)
                t_ref[r, quad, put + low : put + high, :] = total

    def total_of(u, parity, quad):
        total = None
        for part in range(4):
            row = jnp.broadcast_to(v_ref[4 * quad + part, pl.ds(2 * u + parity, 1), :], (blocks, window))
            total = row if total is None else jnp.where(owner >= part, row, total)
        return pltpu.roll(total, 8, 1, stride=8, stride_axis=0)

    def expand(i):
        start = 2 * blocks * i
        here = pl.ds(start if isinstance(i, int) else pl.multiple_of(start, 2 * blocks), 2 * blocks)
        for parity in range(2):
            for quad in range(span // 4):
                totals = [next_ref[parity, quad], total_of(2 * i + 1, parity, quad), total_of(2 * i + 2, parity, quad)]
                next_ref[parity, quad] = totals[2]
                for tap in (parity, 2 + parity):
                    values = jnp.concatenate(totals[tap // 2 : tap // 2 + 2], axis=0)
                    high = values.astype(bf16)
                    low = ((values - high.astype(f32)) * volume_low).astype(f8)
                    full = (values * volume_full).astype(f8)
                    cell16 = window * (4 * quad + tap)
                    l_ref[here, cell16 : cell16 + window] = high
                    l8_ref[here, 2 * cell16 : 2 * cell16 + window] = low
                    l8_ref[here, 2 * cell16 + window : 2 * cell16 + 2 * window] = full

    for parity in range(2):
        for quad in range(span // 4):
            next_ref[parity, quad] = total_of(0, parity, quad)

    def prepare(i, carry):
        expand(i)
        for r in range(2):
            widen(0, 2 * i + r)
        return carry

    lax.fori_loop(0, 8, prepare, 0, unroll=2)

    def build(i, slot):
        for tap in range(-1, 4 if i < 6 else 1):
            targets = [(tap, 0)] * (tap >= 0) + [(tap + 1, 1)] * (tap < 3)
            targets = [(t, p) for t, p in targets if i < 6 or t == 0]
            for four in range(rots // 4):
                for quad in range(6):
                    moved = []
                    for r in range(4 * four, 4 * four + 4):
                        row = t_ref[r, quad, 4 * i + tap + 1 : 4 * i + tap + 2, :]
                        moved.append(pltpu.roll(jnp.broadcast_to(row, (8, window)), 0, 1, stride=1, stride_axis=0))
                    values = jnp.concatenate(moved, axis=0)
                    high = values.astype(bf16)
                    low = ((values - high.astype(f32)) * template_low).astype(f8)
                    full = (values * template_full).astype(f8)
                    for t, p in targets:
                        cell16 = window * (4 * quad + t)
                        at = slice(128 * p + 32 * four, 128 * p + 32 * (four + 1))
                        w_ref[slot, at, cell16 : cell16 + window] = high
                        w8_ref[slot, at, 2 * cell16 : 2 * cell16 + window] = full
                        w8_ref[slot, at, 2 * cell16 + window : 2 * cell16 + 2 * window] = low

    def add_products(steps):
        for left_ref, right_ref, sum_ref, wide in (
            (l_ref, w_ref, acc_ref, window),
            (l8_ref, w8_ref, acc8_ref, 2 * window),
        ):
            left, right = ([], []), []
            for i in steps:
                here = slice(2 * i * blocks, (2 * i + 16) * blocks)
                pieces = [(0, 24 * wide)] if i < 6 else [(4 * quad * wide, wide) for quad in range(6)]
                for start, size in pieces:
                    for plane in range(2):
                        at = start + 16 * plane * wide
                        left[plane].append(left_ref[here, at : at + size])
                    right.append(right_ref[i % 4, :, start : start + size])
            both = jnp.concatenate([jnp.concatenate(part, axis=1) for part in left], axis=0)
            product = lax.dot_general(
                both, jnp.concatenate(right, axis=1), nt, preferred_element_type=f32
            )
            sum_ref[...] = product if 0 in steps else sum_ref[...] + product

    build(0, 0)
    groups = (0,), (1, 2), (3, 4), (5, 6)
    for k, group in enumerate(groups):
        if k == 1:
            for r in range(rots):
                widen(1, r)
        for i in groups[k + 1] if k < 3 else ():
            build(i, i % 4)
            expand(i + 7)
        add_products(group)

    lanes = lax.broadcasted_iota(jnp.int32, (16, window), 1)
    for p in range(2):
        at = slice(128 * p, 128 * (p + 1))
        best = acc_ref[:, at] + acc8_ref[:, at] * (1.0 / (volume_low * template_full))
        for shift in (64, 32, 16, 8):
            best = jnp.maximum(best, pltpu.roll(best, shift, 1))
        best_ref[...] = best
        for plane in range(2):
            score = jnp.zeros((16, window), f32)
            for block in range(13):
                found = best_ref[pl.ds(256 * plane + blocks - 1 - block, 16, stride=blocks), :]
                score = jnp.where(lanes // 8 == block, found, score)
            score_ref[pl.ds(rows * plane + p, 16, stride=2), :] = score
    mine_ref[...] = score_ref[pl.ds(pl.multiple_of(rows * ylo, rows), rows), :][:, :cols]
    theirs_ref[...] = score_ref[pl.ds(pl.multiple_of(rows * (1 - ylo), rows), rows), :][:, :cols]

    def shifted(values, count):
        return pltpu.roll(values, values.shape[0] - count, 0)

    sums = energy
    for count in (1, 2, 4):
        sums = sums + shifted(sums, count)
    sums = sums + shifted(sums, 8) + shifted(sums, 16)
    sums = sums[:rows]
    for count in (1, 2, 4):
        sums = sums + pltpu.roll(sums, window - count, 1)
    sums = sums + pltpu.roll(sums, window - 8, 1) + pltpu.roll(sums, window - 16, 1)
    scale_ref[...] = lax.rsqrt(sums / voxels + epsilon)[:, :cols]


def match_scratch():
    return [
        pltpu.VMEM((span, 64, window), f32),
        pltpu.VMEM((rots, 6, 32, window), f32),
        pltpu.VMEM((28 * blocks, 40 * window), bf16),
        pltpu.VMEM((28 * blocks, 80 * window), f8),
        pltpu.VMEM((4, 256, 24 * window), bf16),
        pltpu.VMEM((4, 256, 48 * window), f8),
        pltpu.VMEM((32 * blocks, 256), f32),
        pltpu.VMEM((32 * blocks, 256), f32),
        pltpu.VMEM((32 * blocks, 128), f32),
        pltpu.VMEM((2 * rows, 128), f32),
        pltpu.VMEM((2, span // 4, blocks, window), f32),
    ]


def shards(volume, template, voxel_maps):
    ylo, z, core = lax.axis_index("ylo"), lax.axis_index("z"), lax.axis_index("core")
    column = lax.axis_index("x") * 2 + lax.axis_index("yhi")
    vmem = pl.BlockSpec(memory_space=pltpu.VMEM)
    hbm = pl.BlockSpec(memory_space=pltpu.HBM)
    smem = pl.BlockSpec(memory_space=pltpu.SMEM)

    copies = jnp.broadcast_to(volume, (16, rows, cols))
    full_rows = lax.all_to_all(copies, group, split_axis=0, concat_axis=0, tiled=True)

    forward, backward = (jnp.asarray(table) for table in dft_tables())
    own, forward = pl.pallas_call(
        rotate_kernel,
        out_shape=[
            jax.ShapeDtypeStruct((half_rows, 128), f32),
            jax.ShapeDtypeStruct((2, 2 * freq_pad, length), bf16),
        ],
        in_specs=[smem, vmem, vmem, hbm],
        out_specs=[vmem] * 2,
        scratch_shapes=[
            pltpu.VMEM((5 * edge, 128), f32),
            pltpu.VMEM((half_rows, 128), jnp.int32),
            pltpu.SemaphoreType.DMA,
        ],
        compiler_params=pltpu.CompilerParams(vmem_limit_bytes=48 * 2**20),
        name="rotate",
    )(core[None].astype(jnp.int32), template, voxel_maps, forward)
    shard = pl.pallas_call(
        whiten_kernel,
        out_shape=jax.ShapeDtypeStruct((1, shard_rows, 128), f32),
        in_specs=[smem, vmem, vmem, hbm, vmem],
        out_specs=vmem,
        scratch_shapes=[
            pltpu.VMEM((2 * rows, length), f32),
            pltpu.VMEM((2 * freq_pad, window), bf16),
            pltpu.VMEM((2 * freq_pad, window), bf16),
            pltpu.SemaphoreType.DMA((2,)),
        ],
        compiler_params=pltpu.CompilerParams(vmem_limit_bytes=50 * 2**20),
        name="whiten",
    )(column[None].astype(jnp.int32), full_rows, forward, backward, own)

    gathered = lax.all_gather(shard, "z", axis=0, tiled=True)
    partner = lax.ppermute(gathered, "core", [(0, 1), (1, 0)])
    place = jnp.stack([z, ylo, core]).astype(jnp.int32)
    mine, theirs, scale = pl.pallas_call(
        match_kernel,
        out_shape=[jax.ShapeDtypeStruct((rows, cols), f32)] * 3,
        in_specs=[smem, vmem, vmem],
        out_specs=[vmem] * 3,
        scratch_shapes=match_scratch(),
        compiler_params=pltpu.CompilerParams(vmem_limit_bytes=44 * 2**20),
        name="match",
    )(place, gathered, partner)
    both = lax.all_gather(theirs, "ylo")
    received = lax.dynamic_index_in_dim(both, 1 - ylo, 0, keepdims=False)
    return (jnp.maximum(mine, received) * scale)[None]


def solution(mesh):
    inner = Mesh(mesh.devices.reshape(2, 16, 2, 4, 2), ("ylo", "z", "core", "x", "yhi"))
    orient, bricks = ("ylo", "z"), ("x", "yhi")
    return jax.shard_map(
        shards,
        mesh=inner,
        in_specs=(P(orient, "core", bricks), P(), P(orient, None)),
        out_specs=P(orient, "core", bricks),
        check_vma=False,
    )
```

```python
import functools
import math

import jax
import jax.numpy as jnp
import ml_dtypes
import numpy as np
from jax import lax
from jax.experimental import pallas as pl
from jax.experimental.pallas import tpu as pltpu
from jax.sharding import Mesh
from jax.sharding import PartitionSpec as P

epsilon = 1e-06
floor_share = 0.1
edge = 24
half = 12
voxels = edge**3
length = 832
cols = 104
window = 128
rows = 32
planes = 32
freqs = length // 2 + 1
freq_pad = 432
group = "ylo", "x", "yhi"
half_rows = 56
shard_rows = 2 * rows + half_rows
span = planes // 2 + edge
rots = 16
blocks = 16
depth = 32 * edge
f32 = jnp.float32
bf16 = jnp.bfloat16
f8 = jnp.float8_e4m3fn
volume_full, volume_low = 2.0**2, 2.0**11
template_full, template_low = 2.0**8, 2.0**17
nt = (((1,), (1,)), ((), ()))
tn = (((0,), (0,)), ((), ()))


def split_table(table):
    high = table.astype(ml_dtypes.bfloat16)
    low = (table - high.astype(np.float64)).astype(ml_dtypes.bfloat16)
    return high, low


@functools.cache
def dft_tables():
    freq = np.arange(freqs)
    angles = 2.0 * np.pi * ((freq[:, None] * np.arange(length)[None, :]) % length) / length
    forward = np.zeros((2, freq_pad, length))
    forward[0, :freqs] = np.cos(angles)
    forward[1, :freqs] = np.sin(angles)
    counts = np.where((freq == 0) | (freq == freqs - 1), 1.0, 2.0)[:, None] / math.sqrt(length)
    padded = np.zeros((2, freq_pad, length + edge))
    padded[0, :freqs, half : half + length] = np.cos(angles) * counts
    padded[1, :freqs, half : half + length] = np.sin(angles) * counts
    forward = forward.reshape(2 * freq_pad, length)
    padded = padded.reshape(2 * freq_pad, length + edge)
    bricks = length // cols
    backward = np.stack([padded[:, cols * j : cols * j + window] for j in range(bricks)])
    return np.stack(split_table(forward)), np.stack(split_table(backward))


def split(values):
    high = values.astype(bf16)
    low = (values - high.astype(f32)).astype(bf16)
    return high, low


def cells_of(a, b):
    if a < 20:
        return [(half * (a // 5) + b, edge * (a % 5), 0, edge)]
    if b < 8:
        return [(48 + b, edge * (a - 20), 0, edge)]
    if a < 22:
        return [(48 + 4 * (a - 20) + b - 8, 96, 0, edge)]
    return [(half * j + b - 4 * (a - 22), 120, 8 * j, 8) for j in range(3)]


def rotate_kernel(core_ref, template_ref, map_ref, f_hbm, out_ref, f_ref, normed_ref, index_ref, sem):
    copy = pltpu.make_async_copy(f_hbm, f_ref, sem)
    copy.start()
    values = template_ref[...]
    centred = values - jnp.sum(values) / voxels
    normed = centred / jnp.sqrt(jnp.sum(centred * centred) + epsilon)
    normed_ref[...] = jnp.zeros_like(normed_ref)
    for a in range(edge):
        at = slice(edge * (a // 5), edge * (a // 5 + 1))
        normed_ref[at, edge * (a % 5) : edge * (a % 5 + 1)] = normed[a]
    index_ref[...] = jnp.full_like(index_ref, -1)

    for core in range(2):

        @pl.when(core_ref[0] == core)
        def place():
            for a in range(edge):
                for b in range(half):
                    start = (a * edge + half * core + b) * edge
                    for at, lane, first, width in cells_of(a, b):
                        index_ref[at : at + 1, lane : lane + width] = map_ref[
                            0:1, start + first : start + first + width
                        ]

    def gather(i, carry):
        at = pl.ds(pl.multiple_of(8 * i, 8), 8)
        index = index_ref[at, :]
        source = jnp.maximum(index, 0)
        a = source // (edge * edge)
        rest = source - a * (edge * edge)
        b = rest // edge
        c = rest - b * edge
        group = a // 5
        lane = (a - 5 * group) * edge + c
        high = jnp.where(index < 0, -1, group * edge + b)
        totals = [jnp.zeros((8, 128), f32) for _ in range(4)]
        for row in range(5 * edge):
            table = jnp.broadcast_to(normed_ref[row : row + 1, :], (8, 128))
            found = jnp.take_along_axis(table, lane, axis=1, mode="promise_in_bounds")
            totals[row % 4] = jnp.where(high == row, found, totals[row % 4])
        out_ref[at, :] = (totals[0] + totals[1]) + (totals[2] + totals[3])
        return carry

    lax.fori_loop(0, half_rows // 8, gather, 0, unroll=7)
    copy.wait()


def whiten_kernel(place_ref, rows_ref, f_ref, b_hbm, own_ref, out_ref, x_ref, bh_ref, bl_ref, sems):
    column = place_ref[0]
    copies = [
        pltpu.make_async_copy(b_hbm.at[0, column], bh_ref, sems.at[0]),
        pltpu.make_async_copy(b_hbm.at[1, column], bl_ref, sems.at[1]),
    ]
    for copy in copies:
        copy.start()
    out_ref[0, 2 * rows :, :] = own_ref[...]
    for plane in range(2):
        for j in range(length // cols):
            x_ref[rows * plane : rows * (plane + 1), cols * j : cols * (j + 1)] = rows_ref[
                plane * 8 + j
            ]
    xh, xl = split(x_ref[...])
    spec = (
        lax.dot_general(f_ref[0], xh, nt, preferred_element_type=f32)
        + lax.dot_general(f_ref[0], xl, nt, preferred_element_type=f32)
        + lax.dot_general(f_ref[1], xh, nt, preferred_element_type=f32)
    )
    real = spec[:freq_pad]
    imag = spec[freq_pad:]
    power = real * real + imag * imag
    k = lax.broadcasted_iota(jnp.int32, power.shape, 0)
    before = jnp.where(k == 0, power[1:2], pltpu.roll(power, 1, 0))
    after = jnp.where(k == freqs - 1, power[freqs - 2 : freqs - 1], pltpu.roll(power, freq_pad - 1, 0))
    total = 2.0 * jnp.sum(power, axis=0, keepdims=True) - power[0:1] - power[freqs - 1 : freqs]
    smoothed = (before + power + after) / 3.0 + floor_share * (total / length) + epsilon
    weights = lax.rsqrt(smoothed)
    wh, wl = split(jnp.concatenate([real * weights, imag * weights], axis=0))
    copies[0].wait()
    copies[1].wait()
    out_ref[0, : 2 * rows, :] = (
        lax.dot_general(wh, bh_ref[...], tn, preferred_element_type=f32)
        + lax.dot_general(wl, bh_ref[...], tn, preferred_element_type=f32)
        + lax.dot_general(wh, bl_ref[...], tn, preferred_element_type=f32)
    )


def match_kernel(
    where_ref, own_ref, other_ref, mine_ref, theirs_ref, scale_ref, v_ref, t_ref, l_ref, l8_ref, w_ref, w8_ref, acc_ref, acc8_ref, best_ref, score_ref, next_ref
):
    z0 = where_ref[0]
    ylo = where_ref[1]
    core = where_ref[2]
    first = (core == 0).astype(f32)

    def load_plane(j, energy):
        plane = z0 - half + j
        valid = jnp.logical_and(plane >= 0, plane < planes).astype(f32)
        plane = jnp.clip(plane, 0, planes - 1)
        z = plane % 16
        start = pl.multiple_of((plane // 16) * rows, rows)
        near = other_ref[z, pl.ds(start, rows), :]
        v_ref[j, half : half + rows, :] = own_ref[z, pl.ds(start, rows), :] * valid
        v_ref[j, 0:half, :] = near[rows - half :] * (valid * (1.0 - first))
        v_ref[j, half + rows : 56, :] = near[:half] * (valid * first)
        v_ref[j, 56:, :] = jnp.zeros((8, window), f32)
        full = v_ref[j, :56, :]
        v_ref[j, :56, :] = pltpu.roll(full, (j % 4) * 32, 1)
        inside = jnp.logical_and(j >= 16 * ylo, j < 16 * ylo + edge).astype(f32)
        return energy + full * full * inside

    energy = lax.fori_loop(0, span, load_plane, jnp.zeros((56, window), f32), unroll=8)

    lane = lax.broadcasted_iota(jnp.int32, (blocks, window), 1)
    place = lax.broadcasted_iota(jnp.int32, (blocks, window), 0)
    owner = ((lane + 8 * place + 8) & (window - 1)) // 32
    cell = lax.broadcasted_iota(jnp.int32, (half, window), 1)

    t_ref[:, :, :8, :] = jnp.zeros((rots, 6, 8, window), f32)
    t_ref[:, :, 24:, :] = jnp.zeros((rots, 6, 8, window), f32)

    def placed(total, source, lane_from, lane_to, width):
        moved = pltpu.roll(source, (lane_to - lane_from) % window, 1)
        at = cell[: source.shape[0]]
        return jnp.where(jnp.logical_and(at >= lane_to, at < lane_to + width), moved, total)

    def widen(k, r):
        mine = core == k
        put = 1 + half * k
        for quad in range(6):
            for low, high in ((0, 8), (8, half)) if quad == 5 else ((0, half),):
                total = jnp.zeros((high - low, window), f32)
                for part in range(4):
                    for at, lane_from, c, width in cells_of(4 * quad + part, low):
                        at = slice(2 * rows + at, 2 * rows + at + high - low)
                        source = jnp.where(mine, own_ref[r, at, :], other_ref[r, at, :])
                        total = placed(total, source, lane_from, 32 * part + c, width)
                t_ref[r, quad, put + low : put + high, :] = total

    def total_of(u, parity, quad):
        total = None
        for part in range(4):
            row = jnp.broadcast_to(v_ref[4 * quad + part, pl.ds(2 * u + parity, 1), :], (blocks, window))
            total = row if total is None else jnp.where(owner >= part, row, total)
        return pltpu.roll(total, 8, 1, stride=8, stride_axis=0)

    def expand(i):
        start = 2 * blocks * i
        here = pl.ds(start if isinstance(i, int) else pl.multiple_of(start, 2 * blocks), 2 * blocks)
        for parity in range(2):
            for quad in range(span // 4):
                totals = [next_ref[parity, quad], total_of(2 * i + 1, parity, quad), total_of(2 * i + 2, parity, quad)]
                next_ref[parity, quad] = totals[2]
                for tap in (parity, 2 + parity):
                    values = jnp.concatenate(totals[tap // 2 : tap // 2 + 2], axis=0)
                    high = values.astype(bf16)
                    low = ((values - high.astype(f32)) * volume_low).astype(f8)
                    full = (values * volume_full).astype(f8)
                    cell16 = window * (4 * quad + tap)
                    l_ref[here, cell16 : cell16 + window] = high
                    l8_ref[here, 2 * cell16 : 2 * cell16 + window] = low
                    l8_ref[here, 2 * cell16 + window : 2 * cell16 + 2 * window] = full

    for parity in range(2):
        for quad in range(span // 4):
            next_ref[parity, quad] = total_of(0, parity, quad)

    def prepare(i, carry):
        expand(i)
        for r in range(2):
            widen(0, 2 * i + r)
        return carry

    lax.fori_loop(0, 8, prepare, 0, unroll=2)

    def build(i, slot):
        for tap in range(-1, 4 if i < 6 else 1):
            targets = [(tap, 0)] * (tap >= 0) + [(tap + 1, 1)] * (tap < 3)
            targets = [(t, p) for t, p in targets if i < 6 or t == 0]
            for four in range(rots // 4):
                for quad in range(6):
                    moved = []
                    for r in range(4 * four, 4 * four + 4):
                        row = t_ref[r, quad, 4 * i + tap + 1 : 4 * i + tap + 2, :]
                        moved.append(pltpu.roll(jnp.broadcast_to(row, (8, window)), 0, 1, stride=1, stride_axis=0))
                    values = jnp.concatenate(moved, axis=0)
                    high = values.astype(bf16)
                    low = ((values - high.astype(f32)) * template_low).astype(f8)
                    full = (values * template_full).astype(f8)
                    for t, p in targets:
                        cell16 = window * (4 * quad + t)
                        at = slice(128 * p + 32 * four, 128 * p + 32 * (four + 1))
                        w_ref[slot, at, cell16 : cell16 + window] = high
                        w8_ref[slot, at, 2 * cell16 : 2 * cell16 + window] = full
                        w8_ref[slot, at, 2 * cell16 + window : 2 * cell16 + 2 * window] = low

    def add_products(steps):
        for left_ref, right_ref, sum_ref, wide in (
            (l_ref, w_ref, acc_ref, window),
            (l8_ref, w8_ref, acc8_ref, 2 * window),
        ):
            left, right = ([], []), []
            for i in steps:
                here = slice(2 * i * blocks, (2 * i + 16) * blocks)
                pieces = [(0, 24 * wide)] if i < 6 else [(4 * quad * wide, wide) for quad in range(6)]
                for start, size in pieces:
                    for plane in range(2):
                        at = start + 16 * plane * wide
                        left[plane].append(left_ref[here, at : at + size])
                    right.append(right_ref[i % 4, :, start : start + size])
            both = jnp.concatenate([jnp.concatenate(part, axis=1) for part in left], axis=0)
            product = lax.dot_general(
                both, jnp.concatenate(right, axis=1), nt, preferred_element_type=f32
            )
            sum_ref[...] = product if 0 in steps else sum_ref[...] + product

    build(0, 0)
    groups = (0,), (1, 2), (3, 4), (5, 6)
    for k, group in enumerate(groups):
        if k == 1:
            for r in range(rots):
                widen(1, r)
        for i in groups[k + 1] if k < 3 else ():
            build(i, i % 4)
            expand(i + 7)
        add_products(group)

    lanes = lax.broadcasted_iota(jnp.int32, (16, window), 1)
    for p in range(2):
        at = slice(128 * p, 128 * (p + 1))
        best = acc_ref[:, at] + acc8_ref[:, at] * (1.0 / (volume_low * template_full))
        for shift in (64, 32, 16, 8):
            best = jnp.maximum(best, pltpu.roll(best, shift, 1))
        best_ref[: 32 * blocks, :] = best
        for plane in range(2):
            score = jnp.zeros((16, window), f32)
            for block in range(13):
                found = best_ref[pl.ds(256 * plane + blocks - 1 - block, 16, stride=blocks), :]
                score = jnp.where(lanes // 8 == block, found, score)
            score_ref[pl.ds(rows * plane + p, 16, stride=2), :] = score
    mine_ref[...] = score_ref[pl.ds(pl.multiple_of(rows * ylo, rows), rows), :][:, :cols]
    theirs_ref[...] = score_ref[pl.ds(pl.multiple_of(rows * (1 - ylo), rows), rows), :][:, :cols]

    def shifted(values, count):
        return pltpu.roll(values, values.shape[0] - count, 0)

    sums = energy
    for count in (1, 2, 4):
        sums = sums + shifted(sums, count)
    sums = sums + shifted(sums, 8) + shifted(sums, 16)
    sums = sums[:rows]
    for count in (1, 2, 4):
        sums = sums + pltpu.roll(sums, window - count, 1)
    sums = sums + pltpu.roll(sums, window - 8, 1) + pltpu.roll(sums, window - 16, 1)
    scale_ref[...] = lax.rsqrt(sums / voxels + epsilon)[:, :cols]


def match_scratch():
    return [
        pltpu.VMEM((span, 64, window), f32),
        pltpu.VMEM((rots, 6, 32, window), f32),
        pltpu.VMEM((28 * blocks, 40 * window), bf16),
        pltpu.VMEM((28 * blocks, 80 * window), f8),
        pltpu.VMEM((4, 256, 24 * window), bf16),
        pltpu.VMEM((4, 256, 48 * window), f8),
        pltpu.VMEM((32 * blocks, 256), f32),
        pltpu.VMEM((32 * blocks, 256), f32),
        pltpu.VMEM((33 * blocks, 128), f32),
        pltpu.VMEM((2 * rows + 8, 128), f32),
        pltpu.VMEM((2, span // 4, blocks, window), f32),
    ]


def shards(volume, template, voxel_maps):
    ylo, z, core = lax.axis_index("ylo"), lax.axis_index("z"), lax.axis_index("core")
    column = lax.axis_index("x") * 2 + lax.axis_index("yhi")
    vmem = pl.BlockSpec(memory_space=pltpu.VMEM)
    hbm = pl.BlockSpec(memory_space=pltpu.HBM)
    smem = pl.BlockSpec(memory_space=pltpu.SMEM)

    copies = jnp.broadcast_to(volume, (16, rows, cols))
    full_rows = lax.all_to_all(copies, group, split_axis=0, concat_axis=0, tiled=True)

    forward, backward = (jnp.asarray(table) for table in dft_tables())
    own, forward = pl.pallas_call(
        rotate_kernel,
        out_shape=[
            jax.ShapeDtypeStruct((half_rows, 128), f32),
            jax.ShapeDtypeStruct((2, 2 * freq_pad, length), bf16),
        ],
        in_specs=[smem, vmem, vmem, hbm],
        out_specs=[vmem] * 2,
        scratch_shapes=[
            pltpu.VMEM((5 * edge, 128), f32),
            pltpu.VMEM((half_rows, 128), jnp.int32),
            pltpu.SemaphoreType.DMA,
        ],
        compiler_params=pltpu.CompilerParams(vmem_limit_bytes=48 * 2**20),
        name="rotate",
    )(core[None].astype(jnp.int32), template, voxel_maps, forward)
    shard = pl.pallas_call(
        whiten_kernel,
        out_shape=jax.ShapeDtypeStruct((1, shard_rows, 128), f32),
        in_specs=[smem, vmem, vmem, hbm, vmem],
        out_specs=vmem,
        scratch_shapes=[
            pltpu.VMEM((2 * rows, length), f32),
            pltpu.VMEM((2 * freq_pad, window), bf16),
            pltpu.VMEM((2 * freq_pad, window), bf16),
            pltpu.SemaphoreType.DMA((2,)),
        ],
        compiler_params=pltpu.CompilerParams(vmem_limit_bytes=50 * 2**20),
        name="whiten",
    )(column[None].astype(jnp.int32), full_rows, forward, backward, own)

    gathered = lax.all_gather(shard, "z", axis=0, tiled=True)
    partner = lax.ppermute(gathered, "core", [(0, 1), (1, 0)])
    place = jnp.stack([z, ylo, core]).astype(jnp.int32)
    mine, theirs, scale = pl.pallas_call(
        match_kernel,
        out_shape=[jax.ShapeDtypeStruct((rows, cols), f32)] * 3,
        in_specs=[smem, vmem, vmem],
        out_specs=[vmem] * 3,
        scratch_shapes=match_scratch(),
        compiler_params=pltpu.CompilerParams(vmem_limit_bytes=44 * 2**20),
        name="match",
    )(place, gathered, partner)
    both = lax.all_gather(theirs, "ylo")
    received = lax.dynamic_index_in_dim(both, 1 - ylo, 0, keepdims=False)
    return (jnp.maximum(mine, received) * scale)[None]


def solution(mesh):
    inner = Mesh(mesh.devices.reshape(2, 16, 2, 4, 2), ("ylo", "z", "core", "x", "yhi"))
    orient, bricks = ("ylo", "z"), ("x", "yhi")
    return jax.shard_map(
        shards,
        mesh=inner,
        in_specs=(P(orient, "core", bricks), P(), P(orient, None)),
        out_specs=P(orient, "core", bricks),
        check_vma=False,
    )
```
